128 devices in a mesh: seq: 8 (over z, core), dp: 16 (over y, x).
Axes of the slice: x: 4, y: 4, z: 4, core: 2. Of those that a mesh axis runs over, the one named last changes fastest.
Arguments:
- activations: bfloat16 [32768, 32768], P(('seq', 'dp')), may hold values from -180 to 180
- start_panel: bfloat16 [32768, 128], P(('seq', 'dp')), may hold values from -6 to 6
Outputs:
- new_panel: bfloat16 [32768, 128], P(('seq', 'dp'))
- sketch: float32 [32768, 128], P(('seq', 'dp'))
The draws below stay inside these ranges and needn't reach their ends.
All inputs are finite; a program needn't handle non-finite values.
Results may differ from the reference program's by a relative error of at most 0.0071.
Values may be sent and summed in bfloat16 or wider, within the bound.
A program may use at most 128 MiB of HBM per device.

```python
import math
import jax
import jax.numpy as jnp
from jax import lax

FEAT = 32768
RANK = 128
NS_STEPS = 12
TOKENS = 32768


def draw_activations(key, part):
    key = jax.random.fold_in(key, 11)
    row_key, col_key, base_key = jax.random.split(key, 3)
    row_scale = jnp.exp(jax.random.uniform(row_key, (TOKENS, 1), jnp.float32) * math.log(10.0))
    base = jnp.clip(jax.random.normal(base_key, (TOKENS, FEAT), jnp.float32), -6.0, 6.0)
    col_scale = jnp.exp(jax.random.uniform(col_key, (1, FEAT), jnp.float32) * math.log(3.0))
    return (base * row_scale * col_scale).astype(jnp.bfloat16)


def draw_start_panel(key, part):
    key = jax.random.fold_in(key, 23)
    values = jnp.clip(jax.random.normal(key, (FEAT, RANK), jnp.float32), -6.0, 6.0)
    return values.astype(jnp.bfloat16)


def setup_inputs(seed: int = 0) -> dict:
    key_list = jax.random.split(jax.random.key(seed), 3)
    activations = draw_activations(jax.random.fold_in(key_list[2], 71), 0)
    start_panel = draw_start_panel(jax.random.fold_in(key_list[2], 71), 0)
    return dict(activations=activations, start_panel=start_panel)


def shrink(ritz_gram):
    shift_mean = jnp.trace(ritz_gram) / RANK
    shifted = ritz_gram - shift_mean * jnp.eye(RANK, dtype=jnp.float32)
    scale_norm = jnp.sqrt(jnp.sum(shifted * shifted)) + 1e-06
    sign_iter = shifted / scale_norm
    for sweep in range(NS_STEPS):
        square = jnp.dot(sign_iter, sign_iter, precision=lax.Precision.HIGHEST)
        cube = jnp.dot(square, sign_iter, precision=lax.Precision.HIGHEST)
        sign_iter = 0.5 * (3.0 * sign_iter - cube)
    positive = 0.5 * (shifted + jnp.dot(shifted, sign_iter, precision=lax.Precision.HIGHEST))
    return (positive, shift_mean)

def reference(activations, start_panel):
    projected = jnp.dot(activations.astype(jnp.float32), start_panel.astype(jnp.float32), preferred_element_type=jnp.float32).astype(jnp.bfloat16)
    pulled = lax.dot_general(activations.astype(jnp.float32), projected.astype(jnp.float32), (((0,), (0,)), ((), ())), preferred_element_type=jnp.float32)
    cross_gram = jnp.dot(pulled.T, pulled, precision=lax.Precision.HIGHEST)
    factor_low = jnp.linalg.cholesky(cross_gram)
    solved = lax.linalg.triangular_solve(factor_low, pulled, left_side=False, lower=True, transpose_a=True)
    new_panel = solved.astype(jnp.bfloat16)
    mapped = jnp.dot(activations.astype(jnp.float32), new_panel.astype(jnp.float32), preferred_element_type=jnp.float32)
    ritz_gram = jnp.dot(mapped.T, mapped, precision=lax.Precision.HIGHEST)
    positive, shift_mean = shrink(ritz_gram)
    sketch = math.sqrt(FEAT) / shift_mean * jnp.dot(new_panel.astype(jnp.float32), positive, precision=lax.Precision.HIGHEST)
    return (new_panel, sketch)
```

```python
import functools
import math

import jax
import jax.numpy as jnp
from jax import lax
from jax.experimental import pallas as pl
from jax.experimental.pallas import tpu as pltpu
from jax.sharding import PartitionSpec as P

NS_STEPS = 12
MESH = pl.DeviceIdType.MESH
F32, BF16 = jnp.float32, jnp.bfloat16
HIGHEST = lax.Precision.HIGHEST
ORDERS = (("x", "y", "z"), ("z", "x", "y"), ("y", "z", "x"))
START_PARTS = ((0, 96), (96, 80), (176, 80))
PANEL_PARTS = ((0, 48), (48, 48), (96, 32))
N_SEMS = 256


def dot(a, b, dims=(((1,), (0,)), ((), ())), precision=None):
    return lax.dot_general(a, b, dims, precision=precision, preferred_element_type=F32)


class Links:
    def __init__(self, send_sems, recv_sems):
        seq, dp = lax.axis_index("seq"), lax.axis_index("dp")
        self.pos = dict(z=seq // 2, c=seq % 2, y=dp // 4, x=dp % 4)
        self.seq, self.dp = seq, dp
        self.send_sems, self.recv_sems, self.used, self.sent = send_sems, recv_sems, 0, []

    def at(self, axis, step):
        return lax.rem(self.pos[axis] + step, 4)

    def device(self, **other):
        p = {**self.pos, **other}
        return (p["z"] * 2 + p["c"], p["y"] * 4 + p["x"])

    def copy(self, src, dst, device):
        i = self.used
        self.used += 1
        made = pltpu.make_async_remote_copy(
            src_ref=src,
            dst_ref=dst,
            send_sem=self.send_sems.at[i],
            recv_sem=self.recv_sems.at[i],
            device_id=device,
            device_id_type=MESH,
        )
        made.start()
        self.sent.append(made)
        return made

    def drain(self):
        for made in self.sent:
            made.wait_send()
        self.sent = []


def gather(links, buf, parts, orders):
    pos, every = links.pos, slice(None)

    def region(part, **index):
        p = {**pos, **index}
        return buf.at[p["c"], p["z"], p["y"], p["x"], pl.ds(*part), :]

    def send(part, axis, step, **index):
        src = region(part, **index)
        return links.copy(src, src, links.device(**{axis: links.at(axis, step)}))

    first, second, third = [], [], [{k: [] for k in (1, 2, 3)} for _ in orders]
    planes = []
    for part, (a, b, c) in zip(parts, orders):
        first.append([send(part, a, k) for k in (1, 3, 2)])
    for o, (part, (a, b, c)) in enumerate(zip(parts, orders)):
        for made in first[o]:
            made.wait_recv()
        row = {a: every}
        second.append([send(part, b, k, **row) for k in (1, 3, 2)])
        for k in (1, 3, 2):
            third[o][k].append(send(part, c, k, **row))
    for j, step in enumerate((1, 3, 2)):
        for o, (part, (a, b, c)) in enumerate(zip(parts, orders)):
            second[o][j].wait_recv()
            row = {a: every, b: links.at(b, 4 - step)}
            for k in (1, 3, 2):
                third[o][k].append(send(part, c, k, **row))
    other = links.device(c=1 - pos["c"])
    for part, (a, b, c) in zip(parts, orders):
        src = region(part, **{a: every, b: every})
        planes.append(links.copy(src, src, other))
    for k in (1, 3, 2):
        for o, (part, (a, b, c)) in enumerate(zip(parts, orders)):
            for made in third[o][k]:
                made.wait_recv()
            src = region(part, **{a: every, b: every, c: links.at(c, 4 - k)})
            planes.append(links.copy(src, src, other))
    return planes


def reduce_scatter(links, produce, work, bufs, parts, orders):
    pos, every = links.pos, slice(None)
    natural = ("z", "y", "x")

    def region(part, **index):
        return work.at[index.get("z", every), index.get("y", every), index.get("x", every), pl.ds(*part), :]

    first = [{k: [] for k in (1, 2, 3)} for _ in orders]
    for step in (1, 3, 2, 0):
        z = links.at("z", step)
        produce(z)
        for o, (part, (c, b, a)) in enumerate(zip(parts, orders)):
            got = bufs[o][0]
            if a == "z":
                if step:
                    first[o][step].append(
                        links.copy(region(part, z=z), got.at[step - 1], links.device(z=z))
                    )
                continue
            for k in (1, 3, 2):
                there = links.at(a, k)
                first[o][k].append(
                    links.copy(region(part, **{a: there, "z": z}), got.at[k - 1, z], links.device(**{a: there}))
                )
    second, third = [], []
    for o, (part, (c, b, a)) in enumerate(zip(parts, orders)):
        got, sum1, got2, sum2, got3 = bufs[o]
        for k in (1, 3, 2):
            for made in first[o][k]:
                made.wait_recv()
        left = [n for n in natural if n != a]

        def add(i, _, a=a, left=left, got=got, sum1=sum1, part=part):
            u, v = i // 4, i % 4
            index = {left[0]: u, left[1]: v, a: pos[a]}
            total = work[index["z"], index["y"], index["x"], pl.ds(*part), :].astype(F32)
            for k in range(3):
                total += got[k, u, v].astype(F32)
            sum1[u, v] = total.astype(BF16)
            return _

        lax.fori_loop(0, 16, add, 0)
        lead = left.index(b) == 0
        made2 = []
        for k in (1, 3, 2):
            there = links.at(b, k)
            src = sum1.at[there] if lead else sum1.at[:, there]
            made2.append(links.copy(src, got2.at[k - 1], links.device(**{b: there})))
        second.append(made2)
    for o, (part, (c, b, a)) in enumerate(zip(parts, orders)):
        got, sum1, got2, sum2, got3 = bufs[o]
        for made in second[o]:
            made.wait_recv()
        left = [n for n in natural if n != a]
        lead = left.index(b) == 0

        def add2(v, _, sum1=sum1, sum2=sum2, got2=got2, lead=lead, b=b):
            total = (sum1[pos[b], v] if lead else sum1[v, pos[b]]).astype(F32)
            for k in range(3):
                total += got2[k, v].astype(F32)
            sum2[v] = total.astype(BF16)
            return _

        lax.fori_loop(0, 4, add2, 0)
        made3 = []
        for k in (1, 3, 2):
            there = links.at(c, k)
            made3.append(links.copy(sum2.at[there], got3.at[k - 1], links.device(**{c: there})))
        third.append(made3)
    totals = []
    for o, (part, (c, b, a)) in enumerate(zip(parts, orders)):
        got, sum1, got2, sum2, got3 = bufs[o]
        for made in third[o]:
            made.wait_recv()
        total = sum2[pos[c]].astype(F32)
        for k in range(3):
            total += got3[k].astype(F32)
        totals.append(total)
    return totals


def factor_steps(work, first, last):
    lane = lax.broadcasted_iota(jnp.int32, (8, 128), 1)
    row = lax.broadcasted_iota(jnp.int32, (8, 1), 0)

    def panel_step(p, _):
        start = pl.multiple_of(p * 8, 8)
        panel = work[pl.ds(start, 8), :]
        left = panel[:, :128]
        cols = [jnp.sum(jnp.where(lane == start + k, left, 0.0), axis=1, keepdims=True) for k in range(8)]
        scale = jnp.zeros((8, 1), F32)
        for k in range(8):
            pivot = cols[k][k : k + 1]
            scale = jnp.where(row == k, pivot, scale)
            below = jnp.where(row > k, cols[k] / pivot, 0.0)
            panel = panel - below * panel[k : k + 1]
            for m in range(k + 1, 8):
                cols[m] = cols[m] - below * cols[m][k : k + 1]
        panel = panel / jnp.sqrt(scale)
        work[pl.ds(start, 8), :] = panel
        rest = jnp.where(lane >= start + 8, panel[:, :128], 0.0)
        work[...] = work[...] - dot(rest, panel, (((0,), (0,)), ((), ())), HIGHEST)
        return _

    lax.fori_loop(first, last, panel_step, 0)


def kernel(stop, act, start, new_ref, sketch_ref, a_v, s_all, t_all, out_d, in_d, work, fac, proj_t,
           h_all, h_in, h_mid, h_out, *rest):
    bufs = [rest[5 * o : 5 * o + 5] for o in range(3)]
    local_sem, send_sems, recv_sems = rest[15:]
    links = Links(send_sems, recv_sems)
    pos = links.pos
    c, z, y, x = pos["c"], pos["z"], pos["y"], pos["x"]
    chunk = 4096

    load_s = pltpu.make_async_copy(start, s_all.at[c, z, y, x], local_sem.at[8])
    load_s.start()
    loads = []
    for i in range(8):
        cols = pl.ds(i * chunk, chunk)
        loads.append(pltpu.make_async_copy(act.at[:, cols], a_v.at[:, cols], local_sem.at[i]))
        loads[-1].start()

    barrier = pltpu.get_barrier_semaphore()
    mates = [(lax.rem(links.seq + k, 8), links.dp) for k in range(1, 8)]
    plane = [(links.seq, lax.rem(links.dp + k, 16)) for k in range(1, 16)]
    for device in mates + plane:
        pl.semaphore_signal(barrier, 1, device_id=device, device_id_type=MESH)
    pl.semaphore_wait(barrier, len(mates) + len(plane))

    load_s.wait()
    planes = gather(links, s_all, START_PARTS, ORDERS)
    for load in loads:
        load.wait()

    def project(colour):
        def body(i, total):
            cols = pl.ds(pl.multiple_of((i * 2 + colour) * chunk, chunk), chunk)
            return total + dot(a_v[:, cols], s_all[colour, i].reshape(chunk, 128))
        return body

    total = lax.fori_loop(0, 4, project(c), jnp.zeros((256, 128), F32))
    for made in planes:
        made.wait_recv()
    total = lax.fori_loop(0, 4, project(1 - c), total)
    proj_t[...] = total.T.astype(BF16)
    if stop == 1:
        links.drain()
        new_ref[...] = total.astype(BF16)
        sketch_ref[...] = total
        return

    def block(colour, zz, yx):
        cols = pl.ds(pl.multiple_of((zz * 32 + colour * 16 + yx) * 256, 256), 256)
        return dot(proj_t[...], a_v[:, cols])

    pair = []
    for step in (1, 3, 2, 0):
        zz = links.at("z", step)

        def give(i, _, zz=zz):
            out_d[zz, i // 4, i % 4] = block(1 - c, zz, i).astype(BF16)
            return _

        lax.fori_loop(0, 16, give, 0)
        pair.append(links.copy(out_d.at[zz], in_d.at[zz], links.device(c=1 - c)))

    waiting = iter(pair)

    def produce(zz):
        next(waiting).wait_recv()

        def own(i, _):
            u, v = i // 4, i % 4
            work[zz, u, v] = (block(c, zz, i) + in_d[zz, u, v].astype(F32)).astype(BF16)
            return _

        lax.fori_loop(0, 16, own, 0)

    totals = reduce_scatter(links, produce, work, bufs, PANEL_PARTS, ORDERS)
    pulled_t = jnp.concatenate(totals, axis=0)
    if stop == 2:
        links.drain()
        new_ref[...] = pulled_t.T.astype(BF16)
        sketch_ref[...] = pulled_t.T
        return
    t_all[c, z, y, x] = pulled_t.astype(BF16)
    planes = gather(links, t_all, PANEL_PARTS, ORDERS)

    NT = (((1,), (1,)), ((), ()))

    def gather_sums(colour):
        def body(i, sums):
            raw, gram = sums
            for u in range(4):
                piece = t_all[colour, i // 4, i % 4, u]
                cols = pl.ds(pl.multiple_of(((i // 4) * 32 + colour * 16 + (i % 4) * 4 + u) * 256, 256), 256)
                raw = raw + dot(a_v[:, cols], piece, NT)
                gram = gram + dot(piece, piece, NT)
            return raw, gram
        return body

    sums = (jnp.zeros((256, 128), F32), jnp.zeros((128, 128), F32))
    sums = lax.fori_loop(0, 16, gather_sums(c), sums)
    for made in planes:
        made.wait_recv()
    raw, gram = lax.fori_loop(0, 16, gather_sums(1 - c), sums)

    rows = lax.broadcasted_iota(jnp.int32, (128, 128), 0)
    cols = lax.broadcasted_iota(jnp.int32, (128, 128), 1)
    eye = rows == cols
    diagonal = jnp.where(eye, gram, 0.0)
    d_row = 1.0 / jnp.sqrt(jnp.sum(diagonal, axis=0, keepdims=True))
    d_col = 1.0 / jnp.sqrt(jnp.sum(diagonal, axis=1, keepdims=True))
    fac[:, :128] = gram * d_row * d_col
    fac[:, 128:] = jnp.where(eye, 1.0, 0.0).astype(F32)
    raw = raw * d_row
    h_all[...] = dot(raw, raw, (((0,), (0,)), ((), ())), HIGHEST)

    seq = links.seq
    made = []
    for k in range(1, 8):
        s = lax.rem(seq + k, 8)
        made.append(links.copy(h_all.at[pl.ds(pl.multiple_of(s * 16, 16), 16)], h_in.at[k - 1], (s, links.dp)))
    factor_steps(fac, 0, 5)
    mine = h_all[pl.ds(pl.multiple_of(seq * 16, 16), 16)]
    for k in range(7):
        made[k].wait_recv()
        mine += h_in[k]
    h_mid[0] = mine
    made = []
    for k in range(1, 16):
        made.append(links.copy(h_mid.at[0], h_mid.at[k], (seq, lax.rem(links.dp + k, 16))))
    factor_steps(fac, 5, 11)
    for m in made:
        m.wait_recv()
    mine = jnp.sum(h_mid[...], axis=0)
    here = pl.ds(pl.multiple_of(seq * 16, 16), 16)
    h_out[here] = mine
    made = []
    for k in range(1, 8):
        made.append(links.copy(h_out.at[here], h_out.at[here], (lax.rem(seq + k, 8), links.dp)))
    factor_steps(fac, 11, 16)
    inverse = fac[:, 128:]
    panel = dot(inverse, pulled_t * d_col, precision=HIGHEST).T.astype(BF16)
    new_ref[...] = panel
    for m in made:
        m.wait_recv()
    ritz = dot(dot(inverse, h_out[...], precision=HIGHEST), inverse, NT, HIGHEST)

    mean = jnp.sum(jnp.where(eye, ritz, 0.0)) / 128
    shifted = ritz - jnp.where(eye, mean, 0.0)
    sign = shifted / (jnp.sqrt(jnp.sum(shifted * shifted)) + 1e-6)

    def sweep(_, sign):
        square = dot(sign, sign, precision=HIGHEST)
        return 0.5 * (3.0 * sign - dot(square, sign, precision=HIGHEST))

    sign = lax.fori_loop(0, NS_STEPS, sweep, sign)
    positive = 0.5 * (shifted + dot(shifted, sign, precision=HIGHEST))
    sketch_ref[...] = math.sqrt(32768) / mean * dot(panel.astype(F32), positive, precision=HIGHEST)
    links.drain()


def local(stop, activations, start_panel):
    scratch = [
        pltpu.VMEM((256, 32768), BF16),
        pltpu.VMEM((2, 4, 4, 4, 256, 128), BF16),
        pltpu.VMEM((2, 4, 4, 4, 128, 256), BF16),
        pltpu.VMEM((4, 4, 4, 128, 256), BF16),
        pltpu.VMEM((4, 4, 4, 128, 256), BF16),
        pltpu.VMEM((4, 4, 4, 128, 256), BF16),
        pltpu.VMEM((128, 256), F32),
        pltpu.VMEM((128, 256), BF16),
        pltpu.VMEM((128, 128), F32),
        pltpu.VMEM((7, 16, 128), F32),
        pltpu.VMEM((16, 16, 128), F32),
        pltpu.VMEM((128, 128), F32),
    ]
    for _, rows in PANEL_PARTS:
        scratch += [
            pltpu.VMEM((3, 4, 4, rows, 256), BF16),
            pltpu.VMEM((4, 4, rows, 256), BF16),
            pltpu.VMEM((3, 4, rows, 256), BF16),
            pltpu.VMEM((4, rows, 256), BF16),
            pltpu.VMEM((3, rows, 256), BF16),
        ]
    scratch += [
        pltpu.SemaphoreType.DMA((9,)),
        pltpu.SemaphoreType.DMA((N_SEMS,)),
        pltpu.SemaphoreType.DMA((N_SEMS,)),
    ]
    return pl.pallas_call(
        functools.partial(kernel, stop),
        out_shape=(
            jax.ShapeDtypeStruct((256, 128), BF16),
            jax.ShapeDtypeStruct((256, 128), F32),
        ),
        in_specs=[pl.BlockSpec(memory_space=pl.ANY)] * 2,
        out_specs=(pl.BlockSpec(memory_space=pltpu.VMEM),) * 2,
        scratch_shapes=scratch,
        compiler_params=pltpu.CompilerParams(
            collective_id=0, has_side_effects=True, vmem_limit_bytes=60 << 20
        ),
        name="subspace",
    )(activations, start_panel)


def solution(mesh, stop=0):
    spec = P(("seq", "dp"), None)
    return jax.shard_map(
        functools.partial(local, stop), mesh=mesh, in_specs=(spec, spec), out_specs=(spec, spec), check_vma=False
    )
```

```python
import math

import jax
import jax.numpy as jnp
from jax import lax
from jax.experimental import pallas as pl
from jax.experimental.pallas import tpu as pltpu
from jax.sharding import PartitionSpec as P

NS_STEPS = 12
MESH = pl.DeviceIdType.MESH
F32, BF16 = jnp.float32, jnp.bfloat16
HIGHEST = lax.Precision.HIGHEST
ORDERS = (("x", "y", "z"), ("z", "x", "y"), ("y", "z", "x"))
START_PARTS = ((0, 96), (96, 80), (176, 80))
PANEL_PARTS = (((0, 48), (48, 32), (80, 48)), ((0, 32), (32, 48), (80, 48)))
N_SEMS = 3 * 42 + 2 * 24 + 5 + 6


def dot(a, b, dims=(((1,), (0,)), ((), ())), precision=None):
    return lax.dot_general(a, b, dims, precision=precision, preferred_element_type=F32)


class Links:
    def __init__(self, sems):
        seq, dp = lax.axis_index("seq"), lax.axis_index("dp")
        self.pos = dict(z=seq // 2, c=seq % 2, y=dp // 4, x=dp % 4)
        self.seq, self.dp = seq, dp
        self.sems, self.used, self.sent = sems, 0, []

    def sem(self):
        self.used += 1
        return self.used - 1

    def at(self, axis, step):
        return lax.rem(self.pos[axis] + step, 4)

    def device(self, **other):
        p = {**self.pos, **other}
        return (p["z"] * 2 + p["c"], p["y"] * 4 + p["x"])

    def copy(self, src, dst, device, send, recv):
        pltpu.make_async_remote_copy(
            src_ref=src,
            dst_ref=dst,
            send_sem=self.sems.at[send],
            recv_sem=self.sems.at[recv],
            device_id=device,
            device_id_type=MESH,
        ).start()

    def wait(self, sem, like):
        pltpu.make_async_copy(like, like, self.sems.at[sem]).wait()

    def drain(self):
        for sem, like in self.sent:
            self.wait(sem, like)


def gather(links, buf, parts, orders, handed, half=()):
    pos, every, three, two = links.pos, slice(None), pl.ds(0, 3), pl.ds(0, 2)
    halves = {1: pl.ds(0, 2), 3: pl.ds(2, 2)}
    other = links.device(c=1 - pos["c"])
    each = list(enumerate(zip(parts, orders)))

    def region(part, **index):
        p = {**pos, **index}
        return buf.at[(p["c"], p["z"], p["y"], p["x"], *half, pl.ds(*part), slice(None))]

    sends = [[links.sem() for _ in range(5)] for _ in orders]
    gets = [[links.sem() for _ in range(9)] for _ in orders]
    for o, (part, (a, b, c)) in each:
        sizes = ({a: three}, {a: every, b: three}, {a: every, b: every, c: two}, {a: every, b: every}, {a: every, b: every, c: every})
        links.sent += [(sem, region(part, **size)) for sem, size in zip(sends[o], sizes)]
        handed.append((gets[o][8], region(part, **sizes[4])))
    rows = [[] for _ in orders]

    def send(o, kind, get, axis, step, **index):
        src = region(parts[o], **index)
        links.copy(src, src, links.device(**{axis: links.at(axis, step)}), sends[o][kind], gets[o][get])

    def wait(o, get, **size):
        links.wait(gets[o][get], region(parts[o], **size))

    def spread(o, row):
        a, b, c = orders[o]
        rows[o].append(row)
        for k in (1, 3):
            send(o, 2, 2 + len(rows[o]), c, k, **row)

    def forward(o, j):
        a, b, c = orders[o]
        wait(o, 3 + j, **{a: every, c: two})
        for k in (1, 3):
            send(o, 3, 7, c, k, **{**rows[o][j], a: halves[k], c: links.at(c, 4 - k)})

    def hand(o, **index):
        a, b, c = orders[o]
        src = region(parts[o], **{a: every, b: every, **index})
        links.copy(src, src, other, sends[o][4], gets[o][8])

    for o, (part, (a, b, c)) in each:
        for k in (1, 3, 2):
            send(o, 0, 0, a, k)
    yield
    for o, (part, (a, b, c)) in each:
        wait(o, 0, **{a: three})
        for k in (1, 3, 2):
            send(o, 1, 2 if k == 2 else 1, b, k, **{a: every})
        spread(o, {a: every})
    yield
    for o, (part, (a, b, c)) in each:
        wait(o, 1, **{a: every, b: two})
        for step in (1, 3):
            spread(o, {a: every, b: links.at(b, 4 - step)})
    yield
    for o, _ in each:
        forward(o, 0)
    for o, (part, (a, b, c)) in each:
        wait(o, 2, **{a: every})
        spread(o, {a: every, b: links.at(b, 2)})
        hand(o)
    yield
    for j in (1, 2, 3):
        for o, _ in each:
            forward(o, j)
    for k in (1, 3):
        for o, (part, (a, b, c)) in each:
            hand(o, **{c: links.at(c, 4 - k)})
    yield
    for o, (part, (a, b, c)) in each:
        wait(o, 7, **{a: every, b: every})
        hand(o, **{c: links.at(c, 2)})


class Reduce:
    natural = ("z", "y", "x")
    steps = (2, 1, 3, 0)
    halves = {1: pl.ds(0, 2), 3: pl.ds(2, 2)}

    def __init__(self, links, work, h, bufs, parts, orders):
        self.links, self.work, self.h, self.bufs = links, work, h, bufs
        self.parts, self.orders = parts, orders
        self.each = list(enumerate(zip(parts, orders)))
        self.sends = [[links.sem() for _ in range(4)] for _ in orders]
        self.gets = [[links.sem() for _ in range(4)] for _ in orders]
        two, three = pl.ds(0, 2), pl.ds(0, 3)
        self.sizes = []
        for o, (part, (c, b, a)) in self.each:
            sum1, sum2 = bufs[o][2], bufs[o][4]
            likes = (self.region(part, **{a: 0}), self.region(part, **{a: two}), sum1.at[three], sum2.at[three])
            links.sent += list(zip(self.sends[o], likes))
            self.sizes.append(likes)

    def at(self, part, **index):
        every = slice(None)
        where = [index.get(n, every) for n in self.natural]
        return (*where, self.h, pl.ds(*part), every)

    def region(self, part, **index):
        return self.work.at[self.at(part, **index)]

    def send(self, o, kind, src, dst, axis, to):
        links = self.links
        links.copy(src, dst, links.device(**{axis: to}), self.sends[o][kind], self.gets[o][kind])

    def wait(self, o, kind):
        self.links.wait(self.gets[o][kind], self.sizes[o][kind])

    def start(self, n=None):
        links = self.links
        for o, (part, (c, b, a)) in self.each:
            via = self.bufs[o][0]
            left = "x" if a == "y" else "y"
            if a == "z" and n not in (None, 0):
                continue
            for i, k in enumerate((1, 3)):
                index, dst = {a: links.at(a, 2), left: self.halves[k]}, via.at[i]
                if a != "z" and n is not None:
                    z = links.at("z", self.steps[n])
                    index["z"], dst = z, via.at[i, z]
                self.send(o, 0, self.region(part, **index), dst, a, links.at(a, k))

    def forward(self):
        links, work = self.links, self.work
        for o, (part, (c, b, a)) in self.each:
            via, got = self.bufs[o][:2]
            self.wait(o, 0)
            for i, k in enumerate((1, 3)):
                there = links.at(a, k)
                for u in range(4):
                    for j in range(2):
                        v = 2 * i + j
                        if a == "z":
                            block, piece = dict(z=there, y=v, x=u), via[i, j, u]
                        elif a == "y":
                            block, piece = dict(z=u, y=there, x=v), via[i, u, j]
                        else:
                            block, piece = dict(z=u, y=v, x=there), via[i, u, j]
                        where = self.at(part, **block)
                        work[where] = (work[where].astype(F32) + piece.astype(F32)).astype(BF16)
                self.send(o, 1, self.region(part, **{a: there}), got.at[i], a, there)

    def own(self):
        links, pos = self.links, self.links.pos
        for o, (part, (c, b, a)) in self.each:
            got, sum1, got2 = self.bufs[o][1:4]
            self.wait(o, 1)
            left = [n for n in self.natural if n != a]
            lead = left.index(b) == 0
            for step in (2, 1, 3, 0):
                there = links.at(b, step)
                for w in range(4):
                    u, v = (there, w) if lead else (w, there)
                    mine = self.work[self.at(part, **{a: pos[a], left[0]: u, left[1]: v})].astype(F32)
                    sum1[u, v] = (mine + got[0, u, v].astype(F32) + got[1, u, v].astype(F32)).astype(BF16)
                if step:
                    src = sum1.at[there] if lead else sum1.at[:, there]
                    self.send(o, 2, src, got2.at[step - 1], b, there)

    def last_axis(self):
        links, pos = self.links, self.links.pos
        for o, (part, (c, b, a)) in self.each:
            sum1, got2, sum2, got3 = self.bufs[o][2:]
            self.wait(o, 2)
            lead = [n for n in self.natural if n != a].index(b) == 0
            for step in (2, 1, 3, 0):
                v = links.at(c, step)
                total = (sum1[pos[b], v] if lead else sum1[v, pos[b]]).astype(F32)
                for k in range(3):
                    total += got2[k, v].astype(F32)
                sum2[v] = total.astype(BF16)
                if step:
                    self.send(o, 3, sum2.at[v], got3.at[step - 1], c, v)

    def finish(self):
        totals = []
        for o, (part, (c, b, a)) in self.each:
            sum2, got3 = self.bufs[o][4:]
            self.wait(o, 3)
            total = sum2[self.links.pos[c]].astype(F32)
            for k in range(3):
                total += got3[k].astype(F32)
            totals.append(total)
        return jnp.concatenate(totals, axis=0)


def factor_steps(work, first, last):
    lane = lax.broadcasted_iota(jnp.int32, (8, 128), 1)
    row = lax.broadcasted_iota(jnp.int32, (8, 1), 0)

    def panel_step(p, _):
        start = pl.multiple_of(p * 8, 8)
        panel = work[pl.ds(start, 8), :]
        left = panel[:, :128]
        cols = [jnp.sum(jnp.where(lane == start + k, left, 0.0), axis=1, keepdims=True) for k in range(8)]
        scale = jnp.zeros((8, 1), F32)
        for k in range(8):
            pivot = cols[k][k : k + 1]
            scale = jnp.where(row == k, pivot, scale)
            below = jnp.where(row > k, cols[k] / pivot, 0.0)
            panel = panel - below * panel[k : k + 1]
            for m in range(k + 1, 8):
                cols[m] = cols[m] - below * cols[m][k : k + 1]
        panel = panel / jnp.sqrt(scale)
        work[pl.ds(start, 8), :] = panel
        rest = jnp.where(lane >= start + 8, panel[:, :128], 0.0)
        work[...] = work[...] - dot(rest, panel, (((0,), (0,)), ((), ())), HIGHEST)
        return _

    lax.fori_loop(first, last, panel_step, 0)


def kernel(act, start, new_ref, sketch_ref, a_v, s_all, t_all, out_d, in_d, work, fac, proj_t,
           h_all, h_in, h_mid, h_out, *rest):
    bufs = [[rest[18 * h + 6 * o : 18 * h + 6 * o + 6] for o in range(3)] for h in range(2)]
    local_sem, sems = rest[36:]
    links = Links(sems)
    pos = links.pos
    c, z, y, x = pos["c"], pos["z"], pos["y"], pos["x"]
    chunk = 4096

    load_s = pltpu.make_async_copy(start, s_all.at[c, z, y, x], local_sem.at[8])
    load_s.start()
    loads = []
    for i in range(8):
        cols = pl.ds(i * chunk, chunk)
        loads.append(pltpu.make_async_copy(act.at[:, cols], a_v.at[:, cols], local_sem.at[i]))
        loads[-1].start()

    barrier = pltpu.get_barrier_semaphore()
    near = [links.device(**{axis: links.at(axis, k)}) for axis in ("x", "y", "z") for k in (1, 2, 3)]
    near.append(links.device(c=1 - c))
    for device in near:
        pl.semaphore_signal(barrier, 1, device_id=device, device_id_type=MESH)
    pl.semaphore_wait(barrier, len(near))

    load_s.wait()
    handed = []
    for _ in gather(links, s_all, START_PARTS, ORDERS, handed):
        pass
    for load in loads:
        load.wait()

    def project(colour):
        def body(i, total):
            cols = pl.ds(pl.multiple_of((i * 2 + colour) * chunk, chunk), chunk)
            return total + dot(a_v[:, cols], s_all[colour, i].reshape(chunk, 128))
        return body

    total = lax.fori_loop(0, 4, project(c), jnp.zeros((256, 128), F32))
    for sem, like in handed:
        links.wait(sem, like)
    total = lax.fori_loop(0, 4, project(1 - c), total)
    proj_t[...] = total.T.astype(BF16)

    def block(colour, zz, yx):
        cols = pl.ds(pl.multiple_of((zz * 32 + colour * 16 + yx) * 256, 256), 256)
        return dot(proj_t[...], a_v[:, cols])

    pair = [links.sem() for _ in range(4)]
    pair_sent = links.sem()
    links.sent.append((pair_sent, out_d))
    order = [links.at("z", step) for step in (2, 1, 3, 0)]
    given = []

    def give():
        zz = order[len(given)]
        for i in range(16):
            piece = block(1 - c, zz, i).astype(BF16)
            for h in range(2):
                out_d[zz, i // 4, i % 4, h] = piece[:, h * 128 : h * 128 + 128]
        links.copy(out_d.at[zz], in_d.at[zz], links.device(c=1 - c), pair_sent, pair[len(given)])
        given.append(zz)

    def produce(n):
        while len(given) < min(n + 2, 4):
            give()
        zz = order[n]
        links.wait(pair[n], in_d.at[zz])
        for i in range(16):
            u, v = i // 4, i % 4
            piece = block(c, zz, i)
            for h in range(2):
                mine = piece[:, h * 128 : h * 128 + 128] + in_d[zz, u, v, h].astype(F32)
                work[zz, u, v, h] = mine.astype(BF16)

    handed, pulled_t, gathers = [], [None, None], [None, None]
    sums = [Reduce(links, work, h, bufs[h], PANEL_PARTS[h], ORDERS) for h in range(2)]

    def done(h):
        pulled_t[h] = sums[h].finish()
        t_all[c, z, y, x, h] = pulled_t[h].astype(BF16)
        gathers[h] = gather(links, t_all, PANEL_PARTS[h], ORDERS, handed, (h,))
        next(gathers[h])

    for n in range(4):
        produce(n)
        sums[0].start(n)
    sums[1].start()
    sums[0].forward()
    sums[1].forward()
    sums[0].own()
    sums[1].own()
    sums[0].last_axis()
    sums[1].last_axis()
    done(0)
    done(1)
    next(gathers[0])
    next(gathers[1])
    next(gathers[0])
    next(gathers[1])
    next(gathers[0])
    next(gathers[1])
    for _ in gathers[0]:
        pass
    for _ in gathers[1]:
        pass
    pulled_t = jnp.concatenate(pulled_t, axis=1)

    NT = (((1,), (1,)), ((), ()))

    def gather_sums(colour):
        def body(i, sums):
            raw, gram = sums
            for u in range(16):
                piece = jnp.concatenate([t_all[colour, i, u // 4, u % 4, h] for h in range(2)], axis=1)
                cols = pl.ds(pl.multiple_of((i * 32 + colour * 16 + u) * 256, 256), 256)
                raw = raw + dot(a_v[:, cols], piece, NT)
                gram = gram + dot(piece, piece, NT)
            return raw, gram
        return body

    sums = (jnp.zeros((256, 128), F32), jnp.zeros((128, 128), F32))
    sums = lax.fori_loop(0, 4, gather_sums(c), sums)
    for sem, like in handed:
        links.wait(sem, like)
    raw, gram = lax.fori_loop(0, 4, gather_sums(1 - c), sums)

    rows = lax.broadcasted_iota(jnp.int32, (128, 128), 0)
    cols = lax.broadcasted_iota(jnp.int32, (128, 128), 1)
    eye = rows == cols
    diagonal = jnp.where(eye, gram, 0.0)
    d_row = 1.0 / jnp.sqrt(jnp.sum(diagonal, axis=0, keepdims=True))
    d_col = 1.0 / jnp.sqrt(jnp.sum(diagonal, axis=1, keepdims=True))
    fac[:, :128] = gram * d_row * d_col
    fac[:, 128:] = jnp.where(eye, 1.0, 0.0).astype(F32)
    raw = raw * d_row
    h_all[...] = dot(raw, raw, (((0,), (0,)), ((), ())), HIGHEST)

    seq, dp = links.seq, links.dp
    here = pl.ds(pl.multiple_of(seq * 16, 16), 16)
    sent, got = [links.sem() for _ in range(3)], [links.sem() for _ in range(3)]
    links.sent += [(sent[0], h_in), (sent[1], h_mid.at[pl.ds(1, 15)]), (sent[2], h_in)]
    for k in range(1, 8):
        s = lax.rem(seq + k, 8)
        src = h_all.at[pl.ds(pl.multiple_of(s * 16, 16), 16)]
        links.copy(src, h_in.at[k - 1], (s, dp), sent[0], got[0])
    factor_steps(fac, 0, 5)
    links.wait(got[0], h_in)
    h_mid[0] = h_all[here] + jnp.sum(h_in[...], axis=0)
    for k in range(1, 16):
        links.copy(h_mid.at[0], h_mid.at[k], (seq, lax.rem(dp + k, 16)), sent[1], got[1])
    factor_steps(fac, 5, 11)
    links.wait(got[1], h_mid.at[pl.ds(1, 15)])
    h_out[here] = jnp.sum(h_mid[...], axis=0)
    for k in range(1, 8):
        links.copy(h_out.at[here], h_out.at[here], (lax.rem(seq + k, 8), dp), sent[2], got[2])
    factor_steps(fac, 11, 16)
    inverse = fac[:, 128:]
    panel = dot(inverse, pulled_t * d_col, precision=HIGHEST).T.astype(BF16)
    new_ref[...] = panel
    links.wait(got[2], h_in)
    ritz = dot(dot(inverse, h_out[...], precision=HIGHEST), inverse, NT, HIGHEST)

    mean = jnp.sum(jnp.where(eye, ritz, 0.0)) / 128
    shifted = ritz - jnp.where(eye, mean, 0.0)
    sign = shifted / (jnp.sqrt(jnp.sum(shifted * shifted)) + 1e-6)

    def sweep(_, sign):
        square = dot(sign, sign, precision=HIGHEST)
        return 0.5 * (3.0 * sign - dot(square, sign, precision=HIGHEST))

    sign = lax.fori_loop(0, NS_STEPS, sweep, sign)
    positive = 0.5 * (shifted + dot(shifted, sign, precision=HIGHEST))
    sketch_ref[...] = math.sqrt(32768) / mean * dot(panel.astype(F32), positive, precision=HIGHEST)
    links.drain()


def local(activations, start_panel):
    scratch = [
        pltpu.VMEM((256, 32768), BF16),
        pltpu.VMEM((2, 4, 4, 4, 256, 128), BF16),
        pltpu.VMEM((2, 4, 4, 4, 2, 128, 128), BF16),
        pltpu.VMEM((4, 4, 4, 2, 128, 128), BF16),
        pltpu.VMEM((4, 4, 4, 2, 128, 128), BF16),
        pltpu.VMEM((4, 4, 4, 2, 128, 128), BF16),
        pltpu.VMEM((128, 256), F32),
        pltpu.VMEM((128, 256), BF16),
        pltpu.VMEM((128, 128), F32),
        pltpu.VMEM((7, 16, 128), F32),
        pltpu.VMEM((16, 16, 128), F32),
        pltpu.VMEM((128, 128), F32),
    ]
    for parts in PANEL_PARTS:
        for (_, rows), order in zip(parts, ORDERS):
            along_z = order[2] == "z"
            scratch += [
                pltpu.VMEM((2, 2, 4, rows, 128) if along_z else (2, 4, 2, rows, 128), BF16),
                pltpu.VMEM((2, 4, 4, rows, 128), BF16),
                pltpu.VMEM((4, 4, rows, 128), BF16),
                pltpu.VMEM((3, 4, rows, 128), BF16),
                pltpu.VMEM((4, rows, 128), BF16),
                pltpu.VMEM((3, rows, 128), BF16),
            ]
    scratch += [
        pltpu.SemaphoreType.DMA((9,)),
        pltpu.SemaphoreType.DMA((N_SEMS,)),
    ]
    return pl.pallas_call(
        kernel,
        out_shape=(
            jax.ShapeDtypeStruct((256, 128), BF16),
            jax.ShapeDtypeStruct((256, 128), F32),
        ),
        in_specs=[pl.BlockSpec(memory_space=pl.ANY)] * 2,
        out_specs=(pl.BlockSpec(memory_space=pltpu.VMEM),) * 2,
        scratch_shapes=scratch,
        compiler_params=pltpu.CompilerParams(
            collective_id=0, has_side_effects=True, vmem_limit_bytes=60 << 20
        ),
        name="subspace",
    )(activations, start_panel)


def solution(mesh):
    spec = P(("seq", "dp"), None)
    return jax.shard_map(
        local, mesh=mesh, in_specs=(spec, spec), out_specs=(spec, spec), check_vma=False
    )
```

```python
import math

import jax
import jax.numpy as jnp
from jax import lax
from jax.experimental import pallas as pl
from jax.experimental.pallas import tpu as pltpu
from jax.sharding import PartitionSpec as P

NS_STEPS = 12
MESH = pl.DeviceIdType.MESH
F32, BF16 = jnp.float32, jnp.bfloat16
HIGHEST = lax.Precision.HIGHEST
ORDERS = (("x", "y", "z"), ("z", "x", "y"), ("y", "z", "x"))
PARTS = (((0, 48), (48, 32), (80, 48)), ((0, 32), (32, 48), (80, 48)))
N_SEMS = 4 * 45 + 2 * 24 + 9 + 6


def dot(a, b, dims=(((1,), (0,)), ((), ())), precision=None):
    return lax.dot_general(a, b, dims, precision=precision, preferred_element_type=F32)


class Links:
    def __init__(self, sems):
        seq, dp = lax.axis_index("seq"), lax.axis_index("dp")
        x, y, z, c = dp % 4, dp // 4, seq // 2, seq % 2
        first = c == 0
        self.pos = dict(c=c, x=jnp.where(first, x, y), y=jnp.where(first, y, z), z=jnp.where(first, z, x))
        self.twin = dict(c=1 - c, x=jnp.where(first, y, x), y=jnp.where(first, z, y), z=jnp.where(first, x, z))
        self.seq, self.dp = seq, dp
        self.sems, self.used, self.sent = sems, 0, []

    def sem(self):
        self.used += 1
        return self.used - 1

    def at(self, axis, step):
        return lax.rem(self.pos[axis] + step, 4)

    def device(self, **other):
        p, first = {**self.pos, **other}, self.pos["c"] == 0
        x = jnp.where(first, p["x"], p["z"])
        y = jnp.where(first, p["y"], p["x"])
        z = jnp.where(first, p["z"], p["y"])
        return (z * 2 + p["c"], y * 4 + x)

    def columns(self, colour):
        first = colour == 0
        strides = [jnp.where(first, a, b) for a, b in ((32, 1), (4, 32), (1, 4))]

        def columns(*where):
            place = colour * 16 + sum(i * stride for i, stride in zip(where, strides))
            return pl.ds(pl.multiple_of(place * 256, 256), 256)

        return columns

    def copy(self, src, dst, device, send, recv):
        pltpu.make_async_remote_copy(
            src_ref=src,
            dst_ref=dst,
            send_sem=self.sems.at[send],
            recv_sem=self.sems.at[recv],
            device_id=device,
            device_id_type=MESH,
        ).start()

    def wait(self, sem, like):
        pltpu.make_async_copy(like, like, self.sems.at[sem]).wait()

    def drain(self):
        for sem, like in self.sent:
            self.wait(sem, like)


def gather(links, buf, parts, orders, handed, half=()):
    pos, every, three, two = links.pos, slice(None), pl.ds(0, 3), pl.ds(0, 2)
    halves = {1: pl.ds(0, 2), 3: pl.ds(2, 2)}
    other = links.device(c=1 - pos["c"])
    each = list(enumerate(zip(parts, orders)))

    def region(part, **index):
        p = {**pos, **index}
        return buf.at[(p["c"], p["z"], p["y"], p["x"], *half, pl.ds(*part), slice(None))]

    sends = [[links.sem() for _ in range(5)] for _ in orders]
    gets = [[links.sem() for _ in range(10)] for _ in orders]
    for o, (part, (a, b, c)) in each:
        sizes = ({a: three}, {a: every, b: three}, {a: every, b: every, c: two}, {a: every, b: every}, {a: every, b: every, c: every})
        links.sent += [(sem, region(part, **size)) for sem, size in zip(sends[o], sizes)]
        handed[0].append((gets[o][8], region(part, **{a: every, b: every, c: three})))
        handed[1].append((gets[o][9], region(part, **{a: every, b: every})))
    rows = [[] for _ in orders]

    def send(o, kind, get, axis, step, **index):
        src = region(parts[o], **index)
        links.copy(src, src, links.device(**{axis: links.at(axis, step)}), sends[o][kind], gets[o][get])

    def wait(o, get, **size):
        links.wait(gets[o][get], region(parts[o], **size))

    def spread(o, row):
        a, b, c = orders[o]
        rows[o].append(row)
        for k in (1, 3):
            send(o, 2, 2 + len(rows[o]), c, k, **row)

    def forward(o, j):
        a, b, c = orders[o]
        wait(o, 3 + j, **{a: every, c: two})
        for k in (1, 3):
            send(o, 3, 7, c, k, **{**rows[o][j], a: halves[k], c: links.at(c, 4 - k)})

    def hand(o, step):
        a, b, c = orders[o]
        src = region(parts[o], **{a: every, b: every, c: links.at(c, step)})
        links.copy(src, src, other, sends[o][4], gets[o][9 if step == 2 else 8])

    for o, (part, (a, b, c)) in each:
        for k in (1, 3, 2):
            send(o, 0, 0, a, k)
    yield
    for o, (part, (a, b, c)) in each:
        wait(o, 0, **{a: three})
        for k in (1, 3, 2):
            send(o, 1, 2 if k == 2 else 1, b, k, **{a: every})
        spread(o, {a: every})
    yield
    for o, (part, (a, b, c)) in each:
        wait(o, 1, **{a: every, b: two})
        for step in (1, 3):
            spread(o, {a: every, b: links.at(b, 4 - step)})
    yield
    for o, _ in each:
        forward(o, 0)
    for o, (part, (a, b, c)) in each:
        wait(o, 2, **{a: every})
        spread(o, {a: every, b: links.at(b, 2)})
        hand(o, 0)
    yield
    for j in (1, 2, 3):
        for o, _ in each:
            forward(o, j)
    for k in (1, 3):
        for o, (part, (a, b, c)) in each:
            hand(o, 4 - k)
    yield
    for o, (part, (a, b, c)) in each:
        wait(o, 7, **{a: every, b: every})
        hand(o, 2)


class Reduce:
    natural = ("z", "y", "x")
    steps = (2, 1, 3, 0)
    halves = {1: pl.ds(0, 2), 3: pl.ds(2, 2)}

    def __init__(self, links, work, h, bufs, parts, orders):
        self.links, self.work, self.h, self.bufs = links, work, h, bufs
        self.parts, self.orders = parts, orders
        self.each = list(enumerate(zip(parts, orders)))
        self.sends = [[links.sem() for _ in range(4)] for _ in orders]
        self.gets = [[links.sem() for _ in range(4)] for _ in orders]
        two, three = pl.ds(0, 2), pl.ds(0, 3)
        self.sizes = []
        for o, (part, (c, b, a)) in self.each:
            sum1, sum2 = bufs[o][2], bufs[o][4]
            likes = (self.region(part, **{a: 0}), self.region(part, **{a: two}), sum1.at[three], sum2.at[three])
            links.sent += list(zip(self.sends[o], likes))
            self.sizes.append(likes)

    def at(self, part, **index):
        every = slice(None)
        where = [index.get(n, every) for n in self.natural]
        return (*where, self.h, pl.ds(*part), every)

    def region(self, part, **index):
        return self.work.at[self.at(part, **index)]

    def send(self, o, kind, src, dst, axis, to):
        links = self.links
        links.copy(src, dst, links.device(**{axis: to}), self.sends[o][kind], self.gets[o][kind])

    def wait(self, o, kind):
        self.links.wait(self.gets[o][kind], self.sizes[o][kind])

    def start(self, n=None):
        links = self.links
        for o, (part, (c, b, a)) in self.each:
            via = self.bufs[o][0]
            left = "x" if a == "y" else "y"
            if a == "z" and n not in (None, 0):
                continue
            for i, k in enumerate((1, 3)):
                index, dst = {a: links.at(a, 2), left: self.halves[k]}, via.at[i]
                if a != "z" and n is not None:
                    z = links.at("z", self.steps[n])
                    index["z"], dst = z, via.at[i, z]
                self.send(o, 0, self.region(part, **index), dst, a, links.at(a, k))

    def forward(self):
        links, work = self.links, self.work
        for o, (part, (c, b, a)) in self.each:
            via, got = self.bufs[o][:2]
            self.wait(o, 0)
            for i, k in enumerate((1, 3)):
                there = links.at(a, k)
                for u in range(4):
                    for j in range(2):
                        v = 2 * i + j
                        if a == "z":
                            block, piece = dict(z=there, y=v, x=u), via[i, j, u]
                        elif a == "y":
                            block, piece = dict(z=u, y=there, x=v), via[i, u, j]
                        else:
                            block, piece = dict(z=u, y=v, x=there), via[i, u, j]
                        where = self.at(part, **block)
                        work[where] = (work[where].astype(F32) + piece.astype(F32)).astype(BF16)
                self.send(o, 1, self.region(part, **{a: there}), got.at[i], a, there)

    def own(self):
        links, pos = self.links, self.links.pos
        for o, (part, (c, b, a)) in self.each:
            got, sum1, got2 = self.bufs[o][1:4]
            self.wait(o, 1)
            left = [n for n in self.natural if n != a]
            lead = left.index(b) == 0
            for step in (2, 1, 3, 0):
                there = links.at(b, step)
                for w in range(4):
                    u, v = (there, w) if lead else (w, there)
                    mine = self.work[self.at(part, **{a: pos[a], left[0]: u, left[1]: v})].astype(F32)
                    sum1[u, v] = (mine + got[0, u, v].astype(F32) + got[1, u, v].astype(F32)).astype(BF16)
                if step:
                    src = sum1.at[there] if lead else sum1.at[:, there]
                    self.send(o, 2, src, got2.at[step - 1], b, there)

    def last_axis(self):
        links, pos = self.links, self.links.pos
        for o, (part, (c, b, a)) in self.each:
            sum1, got2, sum2, got3 = self.bufs[o][2:]
            self.wait(o, 2)
            lead = [n for n in self.natural if n != a].index(b) == 0
            for step in (2, 1, 3, 0):
                v = links.at(c, step)
                total = (sum1[pos[b], v] if lead else sum1[v, pos[b]]).astype(F32)
                for k in range(3):
                    total += got2[k, v].astype(F32)
                sum2[v] = total.astype(BF16)
                if step:
                    self.send(o, 3, sum2.at[v], got3.at[step - 1], c, v)

    def finish(self):
        totals = []
        for o, (part, (c, b, a)) in self.each:
            sum2, got3 = self.bufs[o][4:]
            self.wait(o, 3)
            total = sum2[self.links.pos[c]].astype(F32)
            for k in range(3):
                total += got3[k].astype(F32)
            totals.append(total)
        return jnp.concatenate(totals, axis=0)


def over_blocks(links, colour, near, body, state):
    columns = links.columns(colour)
    pos = {n: jnp.where(colour == links.pos["c"], links.pos[n], links.twin[n]) for n in "xyz"}
    pairs = [(dy, dx) for dy in range(4) for dx in range(4)]

    def visit(state, dz, pairs):
        for dy, dx in pairs:
            where = [lax.rem(pos[n] + d, 4) for n, d in zip("zyx", (dz, dy, dx))]
            state = body(state, where, columns(*where))
        return state

    if not near:
        state = visit(state, 2, pairs)
    pairs = [p for p in pairs if (2 not in p) == near]
    return lax.fori_loop(0, 3, lambda i, state: visit(state, i + i // 2, pairs), state)


def gather_and_sum(links, gathers, handed, body, state):
    mine = links.pos["c"]
    state = over_blocks(links, mine, True, body(mine), state)
    for sem, like in handed[0]:
        links.wait(sem, like)
    state = over_blocks(links, 1 - mine, True, body(1 - mine), state)
    for both in gathers:
        for _ in both:
            pass
    state = over_blocks(links, mine, False, body(mine), state)
    for sem, like in handed[1]:
        links.wait(sem, like)
    return over_blocks(links, 1 - mine, False, body(1 - mine), state)


def factor_steps(work, first, last):
    lane = lax.broadcasted_iota(jnp.int32, (8, 128), 1)
    row = lax.broadcasted_iota(jnp.int32, (8, 1), 0)

    def panel_step(p, _):
        start = pl.multiple_of(p * 8, 8)
        panel = work[pl.ds(start, 8), :]
        left = panel[:, :128]
        cols = [jnp.sum(jnp.where(lane == start + k, left, 0.0), axis=1, keepdims=True) for k in range(8)]
        scale = jnp.zeros((8, 1), F32)
        for k in range(8):
            pivot = cols[k][k : k + 1]
            scale = jnp.where(row == k, pivot, scale)
            below = jnp.where(row > k, cols[k] / pivot, 0.0)
            panel = panel - below * panel[k : k + 1]
            for m in range(k + 1, 8):
                cols[m] = cols[m] - below * cols[m][k : k + 1]
        panel = panel / jnp.sqrt(scale)
        work[pl.ds(start, 8), :] = panel
        rest = jnp.where(lane >= start + 8, panel[:, :128], 0.0)
        work[...] = work[...] - dot(rest, panel, (((0,), (0,)), ((), ())), HIGHEST)
        return _

    lax.fori_loop(first, last, panel_step, 0)


def kernel(act, start, new_ref, sketch_ref, a_v, s_all, t_all, out_d, in_d, work, held, fac, proj_t,
           h_all, h_in, h_mid, h_out, *rest):
    bufs = [[rest[18 * h + 6 * o : 18 * h + 6 * o + 6] for o in range(3)] for h in range(2)]
    local_sem, sems = rest[36:]
    links = Links(sems)
    pos = links.pos
    c, z, y, x = pos["c"], pos["z"], pos["y"], pos["x"]
    chunk = 4096

    load_s = []
    for h in range(2):
        rows = pl.ds(h * 128, 128)
        load_s.append(pltpu.make_async_copy(start.at[rows], s_all.at[c, z, y, x, h], local_sem.at[8 + h]))
        load_s[h].start()
    loads = []
    for i in range(8):
        cols = pl.ds(i * chunk, chunk)
        loads.append(pltpu.make_async_copy(act.at[:, cols], a_v.at[:, cols], local_sem.at[i]))
        loads[-1].start()

    barrier = pltpu.get_barrier_semaphore()
    near = [links.device(**{axis: links.at(axis, k)}) for axis in ("x", "y", "z") for k in (1, 2, 3)]
    near.append(links.device(c=1 - c))
    for device in near:
        pl.semaphore_signal(barrier, 1, device_id=device, device_id_type=MESH)
    pl.semaphore_wait(barrier, len(near))

    for load in load_s:
        load.wait()
    handed = [[], []]
    gathers = [gather(links, s_all, PARTS[h], ORDERS, handed, (h,)) for h in range(2)]
    for _ in range(5):
        next(gathers[0])
        next(gathers[1])
    for load in loads:
        load.wait()

    def project(colour):
        def body(total, where, cols):
            piece = s_all[(colour, *where)].reshape(256, 128)
            return total + dot(a_v[:, cols], piece)

        return body

    total = gather_and_sum(links, gathers, handed, project, jnp.zeros((256, 128), F32))
    proj_t[...] = total.T.astype(BF16)

    pair = [links.sem() for _ in range(8)]
    pair_sent = links.sem()
    links.sent.append((pair_sent, out_d))
    order = [links.at("z", step) for step in Reduce.steps]
    order_other = [lax.rem(links.twin["z"] + step, 4) for step in Reduce.steps]

    def plane(colour, zz, store):
        columns = links.columns(colour)
        for i in range(16):
            piece = dot(proj_t[...], a_v[:, columns(zz, i // 4, i % 4)])
            store(i // 4, i % 4, piece[:, :128], piece[:, 128:])

    def give(n):
        zz = order_other[n]

        def store(u, v, *pieces):
            for h in range(2):
                out_d[h, zz, u, v] = pieces[h].astype(BF16)

        plane(1 - c, zz, store)
        for h in range(2):
            src = out_d.at[h, zz]
            given.append((src, in_d.at[h, zz], links.device(c=1 - c), pair_sent, pair[4 * h + n]))

    def own(n):
        zz = order[n]
        links.wait(pair[n], in_d.at[0, zz])
        for m in ((), (), (0,), (1, 2, 3))[n]:
            links.copy(*given[2 * m + 1])

        def store(u, v, first, second):
            work[zz, u, v, 0] = (first + in_d[0, zz, u, v].astype(F32)).astype(BF16)
            held[zz, u, v] = second

        plane(c, zz, store)

    def own_second(n):
        zz = order[n]
        links.wait(pair[4 + n], in_d.at[1, zz])
        for i in range(16):
            u, v = i // 4, i % 4
            work[zz, u, v, 1] = (held[zz, u, v] + in_d[1, zz, u, v].astype(F32)).astype(BF16)

    handed, pulled_t, gathers = [[], []], [None, None], [None, None]
    sums = [Reduce(links, work, h, bufs[h], PARTS[h], ORDERS) for h in range(2)]

    def done(h):
        pulled_t[h] = sums[h].finish()
        t_all[c, z, y, x, h] = pulled_t[h].astype(BF16)
        gathers[h] = gather(links, t_all, PARTS[h], ORDERS, handed, (h,))
        next(gathers[h])

    given = []
    for n in range(4):
        give(n)
        links.copy(*given[2 * n])
    for n in range(4):
        own(n)
        sums[0].start(n)
    sums[0].forward()
    for n in range(4):
        own_second(n)
    sums[1].start()
    sums[0].own()
    sums[1].forward()
    sums[0].last_axis()
    sums[1].own()
    done(0)
    sums[1].last_axis()
    next(gathers[0])
    done(1)
    next(gathers[0])
    next(gathers[1])
    next(gathers[0])
    next(gathers[1])
    next(gathers[0])
    next(gathers[1])
    next(gathers[1])
    pulled_t = jnp.concatenate(pulled_t, axis=1)

    NT = (((1,), (1,)), ((), ()))

    def raw_and_squares(colour):
        def body(sums, where, cols):
            raw, squares = sums
            halves = [t_all[(colour, *where, h)] for h in range(2)]
            for half in halves:
                squares = squares + half.astype(F32) * half.astype(F32)
            return raw + dot(a_v[:, cols], jnp.concatenate(halves, axis=1), NT), squares

        return body

    zeros = (jnp.zeros((256, 128), F32), jnp.zeros((128, 128), F32))
    raw, squares = gather_and_sum(links, gathers, handed, raw_and_squares, zeros)

    rows = lax.broadcasted_iota(jnp.int32, (128, 128), 0)
    cols = lax.broadcasted_iota(jnp.int32, (128, 128), 1)
    eye = rows == cols
    d_col = 1.0 / jnp.sqrt(jnp.sum(squares, axis=1, keepdims=True))
    d_row = jnp.sum(jnp.where(eye, d_col, 0.0), axis=0, keepdims=True)
    raw = raw * d_row
    h_all[...] = dot(raw, raw, (((0,), (0,)), ((), ())), HIGHEST)

    seq, dp = links.seq, links.dp
    here = pl.ds(pl.multiple_of(seq * 16, 16), 16)
    sent, got = [links.sem() for _ in range(3)], [links.sem() for _ in range(3)]
    links.sent += [(sent[0], h_in), (sent[1], h_mid.at[pl.ds(1, 15)]), (sent[2], h_in)]
    for k in range(1, 8):
        s = lax.rem(seq + k, 8)
        src = h_all.at[pl.ds(pl.multiple_of(s * 16, 16), 16)]
        links.copy(src, h_in.at[k - 1], (s, dp), sent[0], got[0])

    def add_gram(i, gram):
        for u in range(16):
            piece = jnp.concatenate([t_all[i // 4, i % 4, u // 4, u % 4, h] for h in range(2)], axis=1)
            gram = gram + dot(piece, piece, NT)
        return gram

    gram = lax.fori_loop(0, 8, add_gram, jnp.zeros((128, 128), F32))
    fac[:, :128] = gram * d_row * d_col
    fac[:, 128:] = jnp.where(eye, 1.0, 0.0).astype(F32)
    links.wait(got[0], h_in)
    h_mid[0] = h_all[here] + jnp.sum(h_in[...], axis=0)
    for k in range(1, 16):
        links.copy(h_mid.at[0], h_mid.at[k], (seq, lax.rem(dp + k, 16)), sent[1], got[1])
    factor_steps(fac, 0, 8)
    links.wait(got[1], h_mid.at[pl.ds(1, 15)])
    h_out[here] = jnp.sum(h_mid[...], axis=0)
    for k in range(1, 8):
        links.copy(h_out.at[here], h_out.at[here], (lax.rem(seq + k, 8), dp), sent[2], got[2])
    factor_steps(fac, 8, 16)
    inverse = fac[:, 128:]
    panel = dot(inverse, pulled_t * d_col, precision=HIGHEST).T.astype(BF16)
    new_ref[...] = panel
    links.wait(got[2], h_in)
    ritz = dot(dot(inverse, h_out[...], precision=HIGHEST), inverse, NT, HIGHEST)

    mean = jnp.sum(jnp.where(eye, ritz, 0.0)) / 128
    shifted = ritz - jnp.where(eye, mean, 0.0)
    sign = shifted / (jnp.sqrt(jnp.sum(shifted * shifted)) + 1e-6)

    def split(a):
        high = a.astype(BF16)
        return high, (a - high.astype(F32)).astype(BF16)

    def product(a, b):
        return dot(a[0], b[0]) + (dot(a[0], b[1]) + dot(a[1], b[0]))

    def sweep(_, sign):
        parts = split(sign)
        square = product(parts, parts)
        return 0.5 * (3.0 * sign - product(split(square), parts))

    sign = lax.fori_loop(0, NS_STEPS, sweep, sign)
    positive = 0.5 * (shifted + dot(shifted, sign, precision=HIGHEST))
    sketch_ref[...] = math.sqrt(32768) / mean * dot(panel.astype(F32), positive, precision=HIGHEST)
    links.drain()


def local(activations, start_panel):
    scratch = [
        pltpu.VMEM((256, 32768), BF16),
        pltpu.VMEM((2, 4, 4, 4, 2, 128, 128), BF16),
        pltpu.VMEM((2, 4, 4, 4, 2, 128, 128), BF16),
        pltpu.VMEM((2, 4, 4, 4, 128, 128), BF16),
        pltpu.VMEM((2, 4, 4, 4, 128, 128), BF16),
        pltpu.VMEM((4, 4, 4, 2, 128, 128), BF16),
        pltpu.VMEM((4, 4, 4, 128, 128), F32),
        pltpu.VMEM((128, 256), F32),
        pltpu.VMEM((128, 256), BF16),
        pltpu.VMEM((128, 128), F32),
        pltpu.VMEM((7, 16, 128), F32),
        pltpu.VMEM((16, 16, 128), F32),
        pltpu.VMEM((128, 128), F32),
    ]
    for parts in PARTS:
        for (_, rows), order in zip(parts, ORDERS):
            along_z = order[2] == "z"
            scratch += [
                pltpu.VMEM((2, 2, 4, rows, 128) if along_z else (2, 4, 2, rows, 128), BF16),
                pltpu.VMEM((2, 4, 4, rows, 128), BF16),
                pltpu.VMEM((4, 4, rows, 128), BF16),
                pltpu.VMEM((3, 4, rows, 128), BF16),
                pltpu.VMEM((4, rows, 128), BF16),
                pltpu.VMEM((3, rows, 128), BF16),
            ]
    scratch += [
        pltpu.SemaphoreType.DMA((10,)),
        pltpu.SemaphoreType.DMA((N_SEMS,)),
    ]
    return pl.pallas_call(
        kernel,
        out_shape=(
            jax.ShapeDtypeStruct((256, 128), BF16),
            jax.ShapeDtypeStruct((256, 128), F32),
        ),
        in_specs=[pl.BlockSpec(memory_space=pl.ANY)] * 2,
        out_specs=(pl.BlockSpec(memory_space=pltpu.VMEM),) * 2,
        scratch_shapes=scratch,
        compiler_params=pltpu.CompilerParams(
            collective_id=0, has_side_effects=True, vmem_limit_bytes=60 << 20
        ),
        name="subspace",
    )(activations, start_panel)


def solution(mesh):
    spec = P(("seq", "dp"), None)
    return jax.shard_map(
        local, mesh=mesh, in_specs=(spec, spec), out_specs=(spec, spec), check_vma=False
    )
```

```python
import math

import jax
import jax.numpy as jnp
from jax import lax
from jax.experimental import pallas as pl
from jax.experimental.pallas import tpu as pltpu
from jax.sharding import PartitionSpec as P

NS_STEPS = 12
MESH = pl.DeviceIdType.MESH
F32, BF16 = jnp.float32, jnp.bfloat16
HIGHEST = lax.Precision.HIGHEST
ORDERS = (("x", "y", "z"), ("z", "x", "y"), ("y", "z", "x"))
PARTS = (((0, 48), (48, 32), (80, 48)), ((0, 32), (32, 48), (80, 48)))
N_SEMS = 4 * 45 + 2 * 33 + 4 + 6


def dot(a, b, dims=(((1,), (0,)), ((), ())), precision=None):
    return lax.dot_general(a, b, dims, precision=precision, preferred_element_type=F32)


class Links:
    def __init__(self, sems):
        seq, dp = lax.axis_index("seq"), lax.axis_index("dp")
        x, y, z, c = dp % 4, dp // 4, seq // 2, seq % 2
        first = c == 0
        self.pos = dict(c=c, x=jnp.where(first, x, y), y=jnp.where(first, y, z), z=jnp.where(first, z, x))
        self.twin = dict(c=1 - c, x=jnp.where(first, y, x), y=jnp.where(first, z, y), z=jnp.where(first, x, z))
        self.seq, self.dp = seq, dp
        self.sems, self.used, self.sent = sems, 0, []

    def sem(self):
        self.used += 1
        return self.used - 1

    def at(self, axis, step):
        return lax.rem(self.pos[axis] + step, 4)

    def device(self, **other):
        p, first = {**self.pos, **other}, self.pos["c"] == 0
        x = jnp.where(first, p["x"], p["z"])
        y = jnp.where(first, p["y"], p["x"])
        z = jnp.where(first, p["z"], p["y"])
        return (z * 2 + p["c"], y * 4 + x)

    def columns(self, colour, apart=False):
        first = colour == 0
        wide, offset = (16, 0) if apart else (32, colour * 16)
        strides = [jnp.where(first, a, b) for a, b in ((wide, 1), (4, wide), (1, 4))]

        def columns(*where):
            place = offset + sum(i * stride for i, stride in zip(where, strides))
            return pl.ds(pl.multiple_of(place * 256, 256), 256)

        return columns

    def copy(self, src, dst, device, send, recv):
        pltpu.make_async_remote_copy(
            src_ref=src,
            dst_ref=dst,
            send_sem=self.sems.at[send],
            recv_sem=self.sems.at[recv],
            device_id=device,
            device_id_type=MESH,
        ).start()

    def wait(self, sem, like):
        pltpu.make_async_copy(like, like, self.sems.at[sem]).wait()

    def drain(self):
        for sem, like in self.sent:
            self.wait(sem, like)


def gather(links, buf, parts, orders, handed, half=()):
    pos, every, three, two = links.pos, slice(None), pl.ds(0, 3), pl.ds(0, 2)
    halves = {1: pl.ds(0, 2), 3: pl.ds(2, 2)}
    other = links.device(c=1 - pos["c"])
    each = list(enumerate(zip(parts, orders)))

    def region(part, **index):
        p = {**pos, **index}
        return buf.at[(p["c"], p["z"], p["y"], p["x"], *half, pl.ds(*part), slice(None))]

    sends = [[links.sem() for _ in range(5)] for _ in orders]
    gets = [[links.sem() for _ in range(10)] for _ in orders]
    for o, (part, (a, b, c)) in each:
        sizes = ({a: three}, {a: every, b: three}, {a: every, b: every, c: two}, {a: every, b: every}, {a: every, b: every, c: every})
        links.sent += [(sem, region(part, **size)) for sem, size in zip(sends[o], sizes)]
        handed[0].append((gets[o][8], region(part, **{a: every, b: every, c: three})))
        handed[1].append((gets[o][9], region(part, **{a: every, b: every})))
    rows = [[] for _ in orders]

    def send(o, kind, get, axis, step, **index):
        src = region(parts[o], **index)
        links.copy(src, src, links.device(**{axis: links.at(axis, step)}), sends[o][kind], gets[o][get])

    def wait(o, get, **size):
        links.wait(gets[o][get], region(parts[o], **size))

    def spread(o, row):
        a, b, c = orders[o]
        rows[o].append(row)
        for k in (1, 3):
            send(o, 2, 2 + len(rows[o]), c, k, **row)

    def forward(o, j):
        a, b, c = orders[o]
        wait(o, 3 + j, **{a: every, c: two})
        for k in (1, 3):
            send(o, 3, 7, c, k, **{**rows[o][j], a: halves[k], c: links.at(c, 4 - k)})

    def hand(o, step):
        a, b, c = orders[o]
        src = region(parts[o], **{a: every, b: every, c: links.at(c, step)})
        links.copy(src, src, other, sends[o][4], gets[o][9 if step == 2 else 8])

    for o, (part, (a, b, c)) in each:
        for k in (1, 3, 2):
            send(o, 0, 0, a, k)
    yield
    for o, (part, (a, b, c)) in each:
        wait(o, 0, **{a: three})
        for k in (1, 3, 2):
            send(o, 1, 2 if k == 2 else 1, b, k, **{a: every})
        spread(o, {a: every})
    yield
    for o, (part, (a, b, c)) in each:
        wait(o, 1, **{a: every, b: two})
        for step in (1, 3):
            spread(o, {a: every, b: links.at(b, 4 - step)})
    yield
    for o, _ in each:
        forward(o, 0)
    for o, (part, (a, b, c)) in each:
        wait(o, 2, **{a: every})
        spread(o, {a: every, b: links.at(b, 2)})
        hand(o, 0)
    yield
    for j in (1, 2, 3):
        for o, _ in each:
            forward(o, j)
    for k in (1, 3):
        for o, (part, (a, b, c)) in each:
            hand(o, 4 - k)
    yield
    for o, (part, (a, b, c)) in each:
        wait(o, 7, **{a: every, b: every})
        hand(o, 2)


class Reduce:
    natural = ("z", "y", "x")
    steps = (2, 1, 3, 0)
    halves = {1: pl.ds(0, 2), 3: pl.ds(2, 2)}

    def __init__(self, links, work, h, bufs, parts, orders):
        self.links, self.work, self.h, self.bufs = links, work, h, bufs
        self.parts, self.orders = parts, orders
        self.each = list(enumerate(zip(parts, orders)))
        self.sends = [[links.sem() for _ in range(4)] for _ in orders]
        self.gets = [[links.sem() for _ in range(4)] for _ in orders]
        self.plane_gets = [[self.gets[o][0]] + [links.sem() for _ in range(3)] for o in range(3)]
        two, three = pl.ds(0, 2), pl.ds(0, 3)
        self.sizes = []
        for o, (part, (c, b, a)) in self.each:
            sum1, sum2 = bufs[o][2], bufs[o][4]
            likes = (self.region(part, **{a: 0}), self.region(part, **{a: two}), sum1.at[three], sum2.at[three])
            links.sent += list(zip(self.sends[o], likes))
            self.sizes.append(likes)

    def at(self, part, **index):
        every = slice(None)
        where = [index.get(n, every) for n in self.natural]
        return (*where, self.h, pl.ds(*part), every)

    def region(self, part, **index):
        return self.work.at[self.at(part, **index)]

    def send(self, o, kind, src, dst, axis, to):
        links = self.links
        links.copy(src, dst, links.device(**{axis: to}), self.sends[o][kind], self.gets[o][kind])

    def wait(self, o, kind):
        self.links.wait(self.gets[o][kind], self.sizes[o][kind])

    def start(self, n):
        links, z = self.links, self.links.at("z", self.steps[n])
        for o, (part, (c, b, a)) in self.each:
            via = self.bufs[o][0]
            left = "x" if a == "y" else "y"
            if a == "z" and n:
                continue
            for i, k in enumerate((1, 3)):
                src = self.region(part, **{"z": z, a: links.at(a, 2), left: self.halves[k]})
                dst = via.at[i] if a == "z" else via.at[i, z]
                to = links.device(**{a: links.at(a, k)})
                links.copy(src, dst, to, self.sends[o][0], self.plane_gets[o][n])

    def forward(self, n):
        links, work, z = self.links, self.work, self.links.at("z", self.steps[n])
        for o, (part, (c, b, a)) in self.each:
            if a == "z" and n:
                continue
            via, got = self.bufs[o][:2]
            like = {a: 0} if a == "z" else {a: 0, "z": 0}
            links.wait(self.plane_gets[o][n], self.region(part, **like))
            for i, k in enumerate((1, 3)):
                there = links.at(a, k)
                for j in range(2):
                    v = 2 * i + j
                    if a == "z":
                        blocks = [(dict(z=there, y=v, x=u), (i, j, u)) for u in range(4)]
                    else:
                        blocks = [(dict(z=z, y=there, x=v) if a == "y" else dict(z=z, y=v, x=there), (i, z, j))]
                    for block, piece in blocks:
                        where = self.at(part, **block)
                        work[where] = (work[where].astype(F32) + via[piece].astype(F32)).astype(BF16)
                index, dst = ({a: there}, got.at[i]) if a == "z" else ({a: there, "z": z}, got.at[i, z])
                self.send(o, 1, self.region(part, **index), dst, a, there)

    def own(self):
        links, pos = self.links, self.links.pos
        for o, (part, (c, b, a)) in self.each:
            got, sum1, got2 = self.bufs[o][1:4]
            self.wait(o, 1)
            left = [n for n in self.natural if n != a]
            lead = left.index(b) == 0
            for step in (2, 1, 3, 0):
                there = links.at(b, step)
                for w in range(4):
                    u, v = (there, w) if lead else (w, there)
                    mine = self.work[self.at(part, **{a: pos[a], left[0]: u, left[1]: v})].astype(F32)
                    sum1[u, v] = (mine + got[0, u, v].astype(F32) + got[1, u, v].astype(F32)).astype(BF16)
                if step:
                    src = sum1.at[there] if lead else sum1.at[:, there]
                    self.send(o, 2, src, got2.at[step - 1], b, there)

    def last_axis(self):
        links, pos = self.links, self.links.pos
        for o, (part, (c, b, a)) in self.each:
            sum1, got2, sum2, got3 = self.bufs[o][2:]
            self.wait(o, 2)
            lead = [n for n in self.natural if n != a].index(b) == 0
            for step in (2, 1, 3, 0):
                v = links.at(c, step)
                total = (sum1[pos[b], v] if lead else sum1[v, pos[b]]).astype(F32)
                for k in range(3):
                    total += got2[k, v].astype(F32)
                sum2[v] = total.astype(BF16)
                if step:
                    self.send(o, 3, sum2.at[v], got3.at[step - 1], c, v)

    def finish(self):
        totals = []
        for o, (part, (c, b, a)) in self.each:
            sum2, got3 = self.bufs[o][4:]
            self.wait(o, 3)
            total = sum2[self.links.pos[c]].astype(F32)
            for k in range(3):
                total += got3[k].astype(F32)
            totals.append(total)
        return jnp.concatenate(totals, axis=0)


def over_blocks(links, colour, near, body, state):
    columns = links.columns(colour)
    pos = {n: jnp.where(colour == links.pos["c"], links.pos[n], links.twin[n]) for n in "xyz"}
    pairs = [(dy, dx) for dy in range(4) for dx in range(4)]

    def visit(state, dz, pairs):
        for dy, dx in pairs:
            where = [lax.rem(pos[n] + d, 4) for n, d in zip("zyx", (dz, dy, dx))]
            state = body(state, where, columns(*where))
        return state

    if not near:
        state = visit(state, 2, pairs)
    pairs = [p for p in pairs if (2 not in p) == near]
    return lax.fori_loop(0, 3, lambda i, state: visit(state, i + i // 2, pairs), state)


def gather_and_sum(links, gathers, handed, body, state):
    mine = links.pos["c"]
    state = over_blocks(links, mine, True, body(mine), state)
    for sem, like in handed[0]:
        links.wait(sem, like)
    state = over_blocks(links, 1 - mine, True, body(1 - mine), state)
    for both in gathers:
        for _ in both:
            pass
    state = over_blocks(links, mine, False, body(mine), state)
    for sem, like in handed[1]:
        links.wait(sem, like)
    return over_blocks(links, 1 - mine, False, body(1 - mine), state)


def factor_steps(work, first, last):
    lane = lax.broadcasted_iota(jnp.int32, (8, 128), 1)
    row = lax.broadcasted_iota(jnp.int32, (8, 1), 0)

    def panel_step(p, _):
        start = pl.multiple_of(p * 8, 8)
        panel = work[pl.ds(start, 8), :]
        left = panel[:, :128]
        cols = [jnp.sum(jnp.where(lane == start + k, left, 0.0), axis=1, keepdims=True) for k in range(8)]
        scale = jnp.zeros((8, 1), F32)
        for k in range(8):
            pivot = cols[k][k : k + 1]
            scale = jnp.where(row == k, pivot, scale)
            below = jnp.where(row > k, cols[k] / pivot, 0.0)
            panel = panel - below * panel[k : k + 1]
            for m in range(k + 1, 8):
                cols[m] = cols[m] - below * cols[m][k : k + 1]
        panel = panel / jnp.sqrt(scale)
        work[pl.ds(start, 8), :] = panel
        rest = jnp.where(lane >= start + 8, panel[:, :128], 0.0)
        work[...] = work[...] - dot(rest, panel, (((0,), (0,)), ((), ())), HIGHEST)
        return _

    lax.fori_loop(first, last, panel_step, 0)


def kernel(act, start, new_ref, positive_ref, a_v, s_all, t_all, a_pair, proj_pair, work, fac, proj_t,
           h_all, h_in, h_mid, h_out, *rest):
    bufs = [[rest[18 * h + 6 * o : 18 * h + 6 * o + 6] for o in range(3)] for h in range(2)]
    local_sem, sems = rest[36:]
    links = Links(sems)
    pos = links.pos
    c, z, y, x = pos["c"], pos["z"], pos["y"], pos["x"]
    chunk = 4096

    load_s = []
    for h in range(2):
        rows = pl.ds(h * 128, 128)
        load_s.append(pltpu.make_async_copy(start.at[rows], s_all.at[c, z, y, x, h], local_sem.at[8 + h]))
        load_s[h].start()
    loads = []
    for i in range(8):
        cols = pl.ds(i * chunk, chunk)
        loads.append(pltpu.make_async_copy(act.at[:, cols], a_v.at[:, cols], local_sem.at[i]))
        loads[-1].start()

    barrier = pltpu.get_barrier_semaphore()
    near = [links.device(**{axis: links.at(axis, k)}) for axis in ("x", "y", "z") for k in (1, 2, 3)]
    near.append(links.device(c=1 - c))
    for device in near:
        pl.semaphore_signal(barrier, 1, device_id=device, device_id_type=MESH)
    pl.semaphore_wait(barrier, len(near))

    twin = links.device(c=1 - c)
    rows_sent, rows_got = links.sem(), links.sem()
    links.sent.append((rows_sent, a_pair))
    for i in range(4):
        src = act.at[:, pl.ds(pl.multiple_of((2 * i + 1 - c) * chunk, chunk), chunk)]
        links.copy(src, a_pair.at[:, pl.ds(i * chunk, chunk)], twin, rows_sent, rows_got)
    for load in load_s:
        load.wait()
    handed = [[], []]
    gathers = [gather(links, s_all, PARTS[h], ORDERS, handed, (h,)) for h in range(2)]
    for _ in range(5):
        next(gathers[0])
        next(gathers[1])
    for load in loads:
        load.wait()

    def project(colour):
        def body(total, where, cols):
            piece = s_all[(colour, *where)].reshape(256, 128)
            return total + dot(a_v[:, cols], piece)

        return body

    total = gather_and_sum(links, gathers, handed, project, jnp.zeros((256, 128), F32))
    proj_t[...] = total.T.astype(BF16)

    proj_sent, proj_got = links.sem(), links.sem()
    links.sent.append((proj_sent, proj_t))
    links.copy(proj_t, proj_pair, twin, proj_sent, proj_got)
    links.wait(rows_got, a_pair)
    links.wait(proj_got, proj_pair)
    columns, columns_pair = links.columns(c), links.columns(c, apart=True)

    def plane(zz):
        for i in range(16):
            where = (zz, i // 4, i % 4)
            piece = dot(proj_t[...], a_v[:, columns(*where)]) + dot(proj_pair[...], a_pair[:, columns_pair(*where)])
            for h in range(2):
                work[(*where, h)] = piece[:, h * 128 : h * 128 + 128].astype(BF16)

    handed, pulled_t, gathers = [[], []], [None, None], [None, None]
    sums = [Reduce(links, work, h, bufs[h], PARTS[h], ORDERS) for h in range(2)]

    def done(h):
        pulled_t[h] = sums[h].finish()
        t_all[c, z, y, x, h] = pulled_t[h].astype(BF16)
        gathers[h] = gather(links, t_all, PARTS[h], ORDERS, handed, (h,))
        next(gathers[h])

    for n, step in enumerate(Reduce.steps):
        plane(links.at("z", step))
        sums[0].start(n)
    for n in range(4):
        sums[1].start(n)
    for n in range(4):
        sums[0].forward(n)
    for n in range(4):
        sums[1].forward(n)
    sums[0].own()
    sums[0].last_axis()
    sums[1].own()
    done(0)
    sums[1].last_axis()
    next(gathers[0])
    done(1)
    next(gathers[0])
    next(gathers[1])
    next(gathers[0])
    next(gathers[1])
    next(gathers[0])
    next(gathers[1])
    next(gathers[1])
    pulled_t = jnp.concatenate(pulled_t, axis=1)

    NT = (((1,), (1,)), ((), ()))

    def raw_and_squares(colour):
        def body(sums, where, cols):
            raw, squares = sums
            halves = [t_all[(colour, *where, h)] for h in range(2)]
            for half in halves:
                squares = squares + half.astype(F32) * half.astype(F32)
            return raw + dot(a_v[:, cols], jnp.concatenate(halves, axis=1), NT), squares

        return body

    zeros = (jnp.zeros((256, 128), F32), jnp.zeros((128, 128), F32))
    raw, squares = gather_and_sum(links, gathers, handed, raw_and_squares, zeros)

    rows = lax.broadcasted_iota(jnp.int32, (128, 128), 0)
    cols = lax.broadcasted_iota(jnp.int32, (128, 128), 1)
    eye = rows == cols
    d_col = 1.0 / jnp.sqrt(jnp.sum(squares, axis=1, keepdims=True))
    d_row = jnp.sum(jnp.where(eye, d_col, 0.0), axis=0, keepdims=True)
    raw = raw * d_row
    h_all[...] = dot(raw, raw, (((0,), (0,)), ((), ())), HIGHEST)

    seq, dp = links.seq, links.dp
    here = pl.ds(pl.multiple_of(seq * 16, 16), 16)
    sent, got = [links.sem() for _ in range(3)], [links.sem() for _ in range(3)]
    links.sent += [(sent[0], h_in), (sent[1], h_mid.at[pl.ds(1, 15)]), (sent[2], h_in)]
    for k in range(1, 8):
        s = lax.rem(seq + k, 8)
        src = h_all.at[pl.ds(pl.multiple_of(s * 16, 16), 16)]
        links.copy(src, h_in.at[k - 1], (s, dp), sent[0], got[0])

    def add_gram(i, gram):
        for u in range(16):
            piece = jnp.concatenate([t_all[i // 4, i % 4, u // 4, u % 4, h] for h in range(2)], axis=1)
            gram = gram + dot(piece, piece, NT)
        return gram

    gram = lax.fori_loop(0, 8, add_gram, jnp.zeros((128, 128), F32))
    fac[:, :128] = gram * d_row * d_col
    fac[:, 128:] = jnp.where(eye, 1.0, 0.0).astype(F32)
    links.wait(got[0], h_in)
    h_mid[0] = h_all[here] + jnp.sum(h_in[...], axis=0)
    for k in range(1, 16):
        links.copy(h_mid.at[0], h_mid.at[k], (seq, lax.rem(dp + k, 16)), sent[1], got[1])
    factor_steps(fac, 0, 8)
    links.wait(got[1], h_mid.at[pl.ds(1, 15)])
    h_out[here] = jnp.sum(h_mid[...], axis=0)
    for k in range(1, 8):
        links.copy(h_out.at[here], h_out.at[here], (lax.rem(seq + k, 8), dp), sent[2], got[2])
    factor_steps(fac, 8, 16)
    inverse = fac[:, 128:]
    panel = dot(inverse, pulled_t * d_col, precision=HIGHEST).T.astype(BF16)
    new_ref[...] = panel
    links.wait(got[2], h_in)
    ritz = dot(dot(inverse, h_out[...], precision=HIGHEST), inverse, NT, HIGHEST)

    mean = jnp.sum(jnp.where(eye, ritz, 0.0)) / 128
    shifted = ritz - jnp.where(eye, mean, 0.0)
    sign = shifted / (jnp.sqrt(jnp.sum(shifted * shifted)) + 1e-6)

    def split(a):
        high = a.astype(BF16)
        return high, (a - high.astype(F32)).astype(BF16)

    def product(a, b):
        return dot(a[0], b[0]) + (dot(a[0], b[1]) + dot(a[1], b[0]))

    def sweep(_, sign):
        parts = split(sign)
        square = product(parts, parts)
        return 0.5 * (3.0 * sign - product(split(square), parts))

    sign = lax.fori_loop(0, NS_STEPS, sweep, sign)
    positive = 0.5 * (shifted + dot(shifted, sign, precision=HIGHEST))
    positive_ref[...] = math.sqrt(32768) / mean * positive
    links.drain()


def finish(panel, positive, new_ref, sketch_ref):
    new_ref[...] = panel[...]
    sketch_ref[...] = dot(panel[...].astype(F32), positive[...], precision=HIGHEST)


def local(activations, start_panel):
    scratch = [
        pltpu.VMEM((256, 32768), BF16),
        pltpu.VMEM((2, 4, 4, 4, 2, 128, 128), BF16),
        pltpu.VMEM((2, 4, 4, 4, 2, 128, 128), BF16),
        pltpu.VMEM((256, 16384), BF16),
        pltpu.VMEM((128, 256), BF16),
        pltpu.VMEM((4, 4, 4, 2, 128, 128), BF16),
        pltpu.VMEM((128, 256), F32),
        pltpu.VMEM((128, 256), BF16),
        pltpu.VMEM((128, 128), F32),
        pltpu.VMEM((7, 16, 128), F32),
        pltpu.VMEM((16, 16, 128), F32),
        pltpu.VMEM((128, 128), F32),
    ]
    for parts in PARTS:
        for (_, rows), order in zip(parts, ORDERS):
            along_z = order[2] == "z"
            scratch += [
                pltpu.VMEM((2, 2, 4, rows, 128) if along_z else (2, 4, 2, rows, 128), BF16),
                pltpu.VMEM((2, 4, 4, rows, 128), BF16),
                pltpu.VMEM((4, 4, rows, 128), BF16),
                pltpu.VMEM((3, 4, rows, 128), BF16),
                pltpu.VMEM((4, rows, 128), BF16),
                pltpu.VMEM((3, rows, 128), BF16),
            ]
    scratch += [
        pltpu.SemaphoreType.DMA((10,)),
        pltpu.SemaphoreType.DMA((N_SEMS,)),
    ]
    panel, positive = pl.pallas_call(
        kernel,
        out_shape=(
            jax.ShapeDtypeStruct((256, 128), BF16),
            jax.ShapeDtypeStruct((128, 128), F32),
        ),
        in_specs=[pl.BlockSpec(memory_space=pl.ANY)] * 2,
        out_specs=(pl.BlockSpec(memory_space=pltpu.VMEM),) * 2,
        scratch_shapes=scratch,
        compiler_params=pltpu.CompilerParams(
            collective_id=0, has_side_effects=True, vmem_limit_bytes=60 << 20
        ),
        name="subspace",
    )(activations, start_panel)
    return pl.pallas_call(
        finish,
        out_shape=(
            jax.ShapeDtypeStruct((256, 128), BF16),
            jax.ShapeDtypeStruct((256, 128), F32),
        ),
        in_specs=[pl.BlockSpec(memory_space=pltpu.VMEM)] * 2,
        out_specs=(pl.BlockSpec(memory_space=pltpu.VMEM),) * 2,
        name="finish",
    )(panel, positive)


def solution(mesh):
    spec = P(("seq", "dp"), None)
    return jax.shard_map(
        local, mesh=mesh, in_specs=(spec, spec), out_specs=(spec, spec), check_vma=False
    )
```

```python
import math

import jax
import jax.numpy as jnp
from jax import lax
from jax.experimental import pallas as pl
from jax.experimental.pallas import tpu as pltpu
from jax.sharding import PartitionSpec as P

NS_STEPS = 12
MESH = pl.DeviceIdType.MESH
F32, BF16 = jnp.float32, jnp.bfloat16
HIGHEST = lax.Precision.HIGHEST
ORDERS = (("x", "y", "z"), ("z", "x", "y"), ("y", "z", "x"))
PARTS = (((0, 48), (48, 32), (80, 48)), ((0, 32), (32, 48), (80, 48)))
N_SEMS = 4 * 48 + 2 * 33 + 4 + 6


def dot(a, b, dims=(((1,), (0,)), ((), ())), precision=None):
    return lax.dot_general(a, b, dims, precision=precision, preferred_element_type=F32)


class Links:
    def __init__(self, sems):
        seq, dp = lax.axis_index("seq"), lax.axis_index("dp")
        x, y, z, c = dp % 4, dp // 4, seq // 2, seq % 2
        first = c == 0
        self.pos = dict(c=c, x=jnp.where(first, x, y), y=jnp.where(first, y, z), z=jnp.where(first, z, x))
        self.twin = dict(c=1 - c, x=jnp.where(first, y, x), y=jnp.where(first, z, y), z=jnp.where(first, x, z))
        self.seq, self.dp = seq, dp
        self.sems, self.used, self.sent = sems, 0, []

    def sem(self):
        self.used += 1
        return self.used - 1

    def at(self, axis, step):
        return lax.rem(self.pos[axis] + step, 4)

    def device(self, **other):
        p, first = {**self.pos, **other}, self.pos["c"] == 0
        x = jnp.where(first, p["x"], p["z"])
        y = jnp.where(first, p["y"], p["x"])
        z = jnp.where(first, p["z"], p["y"])
        return (z * 2 + p["c"], y * 4 + x)

    def columns(self, colour, apart=False):
        first = colour == 0
        wide, offset = (16, 0) if apart else (32, colour * 16)
        strides = [jnp.where(first, a, b) for a, b in ((wide, 1), (4, wide), (1, 4))]

        def columns(*where):
            place = offset + sum(i * stride for i, stride in zip(where, strides))
            return pl.ds(pl.multiple_of(place * 256, 256), 256)

        return columns

    def copy(self, src, dst, device, send, recv):
        pltpu.make_async_remote_copy(
            src_ref=src,
            dst_ref=dst,
            send_sem=self.sems.at[send],
            recv_sem=self.sems.at[recv],
            device_id=device,
            device_id_type=MESH,
        ).start()

    def wait(self, sem, like):
        pltpu.make_async_copy(like, like, self.sems.at[sem]).wait()

    def drain(self):
        for sem, like in self.sent:
            self.wait(sem, like)


def gather(links, buf, parts, orders, handed, half=()):
    pos, every, three, two = links.pos, slice(None), pl.ds(0, 3), pl.ds(0, 2)
    halves = {1: pl.ds(0, 2), 3: pl.ds(2, 2)}
    other = links.device(c=1 - pos["c"])
    each = list(enumerate(zip(parts, orders)))

    def region(part, **index):
        p = {**pos, **index}
        return buf.at[(p["c"], p["z"], p["y"], p["x"], *half, pl.ds(*part), slice(None))]

    sends = [[links.sem() for _ in range(5)] for _ in orders]
    gets = [[links.sem() for _ in range(11)] for _ in orders]
    for o, (part, (a, b, c)) in each:
        sizes = ({a: three}, {a: every, b: three}, {a: every, b: every, c: two}, {a: every, b: every}, {a: every, b: every, c: every})
        links.sent += [(sem, region(part, **size)) for sem, size in zip(sends[o], sizes)]
        handed[0].append((gets[o][8], region(part, **{a: every, b: every, c: three})))
        handed[1].append((gets[o][9], region(part, **{a: every, b: every})))
    rows = [[] for _ in orders]

    def send(o, kind, get, axis, step, **index):
        src = region(parts[o], **index)
        links.copy(src, src, links.device(**{axis: links.at(axis, step)}), sends[o][kind], gets[o][get])

    def wait(o, get, **size):
        links.wait(gets[o][get], region(parts[o], **size))

    def spread(o, row):
        a, b, c = orders[o]
        rows[o].append(row)
        for k in (1, 3):
            send(o, 2, 2 + len(rows[o]), c, k, **row)

    def forward(o, j):
        a, b, c = orders[o]
        wait(o, 3 + j, **{a: every, c: two})
        for k in (1, 3):
            send(o, 3, 10 if j == 3 else 7, c, k, **{**rows[o][j], a: halves[k], c: links.at(c, 4 - k)})

    def hand(o, step, **row):
        a, b, c = orders[o]
        src = region(parts[o], **{a: every, b: every, c: links.at(c, step), **row})
        links.copy(src, src, other, sends[o][4], gets[o][9 if step == 2 else 8])

    for o, (part, (a, b, c)) in each:
        for k in (2, 1, 3):
            send(o, 0, 0, a, k)
    yield
    for o, (part, (a, b, c)) in each:
        wait(o, 0, **{a: three})
        for k in (1, 3, 2):
            send(o, 1, 2 if k == 2 else 1, b, k, **{a: every})
        spread(o, {a: every, b: pos[b]})
    yield
    for o, (part, (a, b, c)) in each:
        wait(o, 1, **{a: every, b: two})
        for step in (1, 3):
            spread(o, {a: every, b: links.at(b, 4 - step)})
    yield
    for o, _ in each:
        forward(o, 0)
    for o, (part, (a, b, c)) in each:
        wait(o, 2, **{a: every})
        spread(o, {a: every, b: links.at(b, 2)})
        hand(o, 0)
    yield
    for j in (1, 2, 3):
        for o, _ in each:
            forward(o, j)
    for k in (1, 3):
        for o, (part, (a, b, c)) in each:
            hand(o, 4 - k)
    yield
    for o, (part, (a, b, c)) in each:
        wait(o, 7, **{a: every, b: three})
        for row in rows[o][:3]:
            hand(o, 2, **row)
    yield
    for o, (part, (a, b, c)) in each:
        wait(o, 10, **{a: every})
        hand(o, 2, **rows[o][3])


class Reduce:
    natural = ("z", "y", "x")
    steps = (2, 1, 3, 0)
    halves = {1: pl.ds(0, 2), 3: pl.ds(2, 2)}

    def __init__(self, links, work, h, bufs, parts, orders):
        self.links, self.work, self.h, self.bufs = links, work, h, bufs
        self.parts, self.orders = parts, orders
        self.each = list(enumerate(zip(parts, orders)))
        self.sends = [[links.sem() for _ in range(4)] for _ in orders]
        self.gets = [[links.sem() for _ in range(4)] for _ in orders]
        self.plane_gets = [[self.gets[o][0]] + [links.sem() for _ in range(3)] for o in range(3)]
        two, three = pl.ds(0, 2), pl.ds(0, 3)
        self.sizes = []
        for o, (part, (c, b, a)) in self.each:
            sum1, sum2 = bufs[o][2], bufs[o][4]
            likes = (self.region(part, **{a: 0}), self.region(part, **{a: two}), sum1.at[three], sum2.at[three])
            links.sent += list(zip(self.sends[o], likes))
            self.sizes.append(likes)

    def at(self, part, **index):
        every = slice(None)
        where = [index.get(n, every) for n in self.natural]
        return (*where, self.h, pl.ds(*part), every)

    def region(self, part, **index):
        return self.work.at[self.at(part, **index)]

    def send(self, o, kind, src, dst, axis, to):
        links = self.links
        links.copy(src, dst, links.device(**{axis: to}), self.sends[o][kind], self.gets[o][kind])

    def wait(self, o, kind):
        self.links.wait(self.gets[o][kind], self.sizes[o][kind])

    def start(self, n):
        links, z = self.links, self.links.at("z", self.steps[n])
        for o, (part, (c, b, a)) in self.each:
            via = self.bufs[o][0]
            left = "x" if a == "y" else "y"
            if a == "z" and n:
                continue
            for i, k in enumerate((1, 3)):
                src = self.region(part, **{"z": z, a: links.at(a, 2), left: self.halves[k]})
                dst = via.at[i] if a == "z" else via.at[i, z]
                to = links.device(**{a: links.at(a, k)})
                links.copy(src, dst, to, self.sends[o][0], self.plane_gets[o][n])

    def forward(self, n):
        links, work, z = self.links, self.work, self.links.at("z", self.steps[n])
        for o, (part, (c, b, a)) in self.each:
            if a == "z" and n:
                continue
            via, got = self.bufs[o][:2]
            like = {a: 0} if a == "z" else {a: 0, "z": 0}
            links.wait(self.plane_gets[o][n], self.region(part, **like))
            for i, k in enumerate((1, 3)):
                there = links.at(a, k)
                for j in range(2):
                    v = 2 * i + j
                    if a == "z":
                        blocks = [(dict(z=there, y=v, x=u), (i, j, u)) for u in range(4)]
                    else:
                        blocks = [(dict(z=z, y=there, x=v) if a == "y" else dict(z=z, y=v, x=there), (i, z, j))]
                    for block, piece in blocks:
                        where = self.at(part, **block)
                        work[where] = (work[where].astype(F32) + via[piece].astype(F32)).astype(BF16)
                index, dst = ({a: there}, got.at[i]) if a == "z" else ({a: there, "z": z}, got.at[i, z])
                self.send(o, 1, self.region(part, **index), dst, a, there)

    def own(self):
        links, pos = self.links, self.links.pos
        for o, (part, (c, b, a)) in self.each:
            got, sum1, got2 = self.bufs[o][1:4]
            self.wait(o, 1)
            left = [n for n in self.natural if n != a]
            lead = left.index(b) == 0
            for step in (2, 1, 3, 0):
                there = links.at(b, step)
                for w in range(4):
                    u, v = (there, w) if lead else (w, there)
                    mine = self.work[self.at(part, **{a: pos[a], left[0]: u, left[1]: v})].astype(F32)
                    sum1[u, v] = (mine + got[0, u, v].astype(F32) + got[1, u, v].astype(F32)).astype(BF16)
                if step:
                    src = sum1.at[there] if lead else sum1.at[:, there]
                    self.send(o, 2, src, got2.at[step - 1], b, there)

    def last_axis(self):
        links, pos = self.links, self.links.pos
        for o, (part, (c, b, a)) in self.each:
            sum1, got2, sum2, got3 = self.bufs[o][2:]
            self.wait(o, 2)
            lead = [n for n in self.natural if n != a].index(b) == 0
            for step in (2, 1, 3, 0):
                v = links.at(c, step)
                total = (sum1[pos[b], v] if lead else sum1[v, pos[b]]).astype(F32)
                for k in range(3):
                    total += got2[k, v].astype(F32)
                sum2[v] = total.astype(BF16)
                if step:
                    self.send(o, 3, sum2.at[v], got3.at[step - 1], c, v)

    def finish(self):
        totals = []
        for o, (part, (c, b, a)) in self.each:
            sum2, got3 = self.bufs[o][4:]
            self.wait(o, 3)
            total = sum2[self.links.pos[c]].astype(F32)
            for k in range(3):
                total += got3[k].astype(F32)
            totals.append(total)
        return jnp.concatenate(totals, axis=0)


def over_blocks(links, colour, near, body, state):
    columns = links.columns(colour)
    pos = {n: jnp.where(colour == links.pos["c"], links.pos[n], links.twin[n]) for n in "xyz"}
    pairs = [(dy, dx) for dy in range(4) for dx in range(4)]

    def visit(state, dz, pairs):
        blocks = []
        for dy, dx in pairs:
            where = [lax.rem(pos[n] + d, 4) for n, d in zip("zyx", (dz, dy, dx))]
            blocks.append((where, columns(*where)))
        return body(state, blocks)

    if not near:
        state = visit(state, 2, pairs)
    pairs = [p for p in pairs if (2 not in p) == near]
    return lax.fori_loop(0, 3, lambda i, state: visit(state, i + i // 2, pairs), state)


def gather_and_sum(links, gathers, handed, body, state):
    mine = links.pos["c"]
    state = over_blocks(links, mine, True, body(mine), state)
    for both in gathers:
        next(both)
    for sem, like in handed[0]:
        links.wait(sem, like)
    state = over_blocks(links, 1 - mine, True, body(1 - mine), state)
    for both in gathers:
        for _ in both:
            pass
    state = over_blocks(links, mine, False, body(mine), state)
    for sem, like in handed[1]:
        links.wait(sem, like)
    return over_blocks(links, 1 - mine, False, body(1 - mine), state)


def factor_steps(work, first, last):
    lane = lax.broadcasted_iota(jnp.int32, (8, 128), 1)
    row = lax.broadcasted_iota(jnp.int32, (8, 1), 0)

    def panel_step(p, _):
        start = pl.multiple_of(p * 8, 8)
        panel = work[pl.ds(start, 8), :]
        left = panel[:, :128]
        cols = [jnp.sum(jnp.where(lane == start + k, left, 0.0), axis=1, keepdims=True) for k in range(8)]
        scale = jnp.zeros((8, 1), F32)
        for k in range(8):
            pivot = cols[k][k : k + 1]
            scale = jnp.where(row == k, pivot, scale)
            below = jnp.where(row > k, cols[k] / pivot, 0.0)
            panel = panel - below * panel[k : k + 1]
            for m in range(k + 1, 8):
                cols[m] = cols[m] - below * cols[m][k : k + 1]
        panel = panel / jnp.sqrt(scale)
        work[pl.ds(start, 8), :] = panel
        rest = jnp.where(lane >= start + 8, panel[:, :128], 0.0)
        work[...] = work[...] - dot(rest, panel, (((0,), (0,)), ((), ())), HIGHEST)
        return _

    lax.fori_loop(first, last, panel_step, 0)


def kernel(act, start, new_ref, positive_ref, a_v, s_all, t_all, a_pair, proj_pair, work, fac, proj_t,
           h_all, h_in, h_mid, h_out, *rest):
    bufs = [[rest[18 * h + 6 * o : 18 * h + 6 * o + 6] for o in range(3)] for h in range(2)]
    local_sem, sems = rest[36:]
    links = Links(sems)
    pos = links.pos
    c, z, y, x = pos["c"], pos["z"], pos["y"], pos["x"]
    chunk = 4096

    load_s = []
    for h in range(2):
        rows = pl.ds(h * 128, 128)
        load_s.append(pltpu.make_async_copy(start.at[rows], s_all.at[c, z, y, x, h], local_sem.at[8 + h]))
        load_s[h].start()
    loads = []
    for i in range(8):
        cols = pl.ds(i * chunk, chunk)
        loads.append(pltpu.make_async_copy(act.at[:, cols], a_v.at[:, cols], local_sem.at[i]))
        loads[-1].start()

    barrier = pltpu.get_barrier_semaphore()
    near = [links.device(**{axis: links.at(axis, k)}) for axis in ("x", "y", "z") for k in (1, 2, 3)]
    near.append(links.device(c=1 - c))
    for device in near:
        pl.semaphore_signal(barrier, 1, device_id=device, device_id_type=MESH)
    pl.semaphore_wait(barrier, len(near))

    twin = links.device(c=1 - c)
    rows_sent, rows_got = links.sem(), links.sem()
    links.sent.append((rows_sent, a_pair))
    for i in range(4):
        src = act.at[:, pl.ds(pl.multiple_of((2 * i + 1 - c) * chunk, chunk), chunk)]
        links.copy(src, a_pair.at[:, pl.ds(i * chunk, chunk)], twin, rows_sent, rows_got)
    for load in load_s:
        load.wait()
    handed = [[], []]
    gathers = [gather(links, s_all, PARTS[h], ORDERS, handed, (h,)) for h in range(2)]
    for _ in range(5):
        next(gathers[0])
        next(gathers[1])
    for load in loads:
        load.wait()

    def project(colour):
        def body(total, blocks):
            pieces = [s_all[(colour, *where)].reshape(256, 128) for where, _ in blocks]
            wide = jnp.concatenate([a_v[:, cols] for _, cols in blocks], axis=1)
            return total + dot(wide, jnp.concatenate(pieces, axis=0))

        return body

    total = gather_and_sum(links, gathers, handed, project, jnp.zeros((256, 128), F32))
    proj_t[...] = total.T.astype(BF16)

    proj_sent, proj_got = links.sem(), links.sem()
    links.sent.append((proj_sent, proj_t))
    links.copy(proj_t, proj_pair, twin, proj_sent, proj_got)
    links.wait(rows_got, a_pair)
    links.wait(proj_got, proj_pair)
    columns, columns_pair = links.columns(c), links.columns(c, apart=True)

    proj_both = jnp.concatenate([proj_t[...], proj_pair[...]], axis=1)

    def plane(zz):
        for i in range(16):
            where = (zz, i // 4, i % 4)
            both = jnp.concatenate([a_v[:, columns(*where)], a_pair[:, columns_pair(*where)]], axis=0)
            piece = dot(proj_both, both)
            for h in range(2):
                work[(*where, h)] = piece[:, h * 128 : h * 128 + 128].astype(BF16)

    handed, pulled_t, gathers = [[], []], [None, None], [None, None]
    sums = [Reduce(links, work, h, bufs[h], PARTS[h], ORDERS) for h in range(2)]

    def done(h):
        pulled_t[h] = sums[h].finish()
        t_all[c, z, y, x, h] = pulled_t[h].astype(BF16)
        gathers[h] = gather(links, t_all, PARTS[h], ORDERS, handed, (h,))
        next(gathers[h])

    for n, step in enumerate(Reduce.steps):
        plane(links.at("z", step))
        sums[0].start(n)
    for n in range(4):
        sums[1].start(n)
    for n in range(4):
        sums[0].forward(n)
    for n in range(4):
        sums[1].forward(n)
    sums[0].own()
    sums[0].last_axis()
    sums[1].own()
    done(0)
    sums[1].last_axis()
    next(gathers[0])
    done(1)
    next(gathers[0])
    next(gathers[1])
    next(gathers[0])
    next(gathers[1])
    next(gathers[0])
    next(gathers[1])
    next(gathers[1])
    pulled_t = jnp.concatenate(pulled_t, axis=1)

    NT = (((1,), (1,)), ((), ()))

    def raw_and_squares(colour):
        def body(sums, blocks):
            raw, squares = sums
            halves = [t_all[(colour, *where, h)] for where, _ in blocks for h in range(2)]
            for half in halves:
                squares = squares + half.astype(F32) * half.astype(F32)
            wide = jnp.concatenate([a_v[:, cols] for _, cols in blocks], axis=1)
            return raw + dot(wide, jnp.concatenate(halves, axis=1), NT), squares

        return body

    zeros = (jnp.zeros((256, 128), F32), jnp.zeros((128, 128), F32))
    raw, squares = gather_and_sum(links, gathers, handed, raw_and_squares, zeros)

    rows = lax.broadcasted_iota(jnp.int32, (128, 128), 0)
    cols = lax.broadcasted_iota(jnp.int32, (128, 128), 1)
    eye = rows == cols
    d_col = 1.0 / jnp.sqrt(jnp.sum(squares, axis=1, keepdims=True))
    d_row = jnp.sum(jnp.where(eye, d_col, 0.0), axis=0, keepdims=True)
    raw = raw * d_row
    h_all[...] = dot(raw, raw, (((0,), (0,)), ((), ())), HIGHEST)

    seq, dp = links.seq, links.dp
    here = pl.ds(pl.multiple_of(seq * 16, 16), 16)
    sent, got = [links.sem() for _ in range(3)], [links.sem() for _ in range(3)]
    links.sent += [(sent[0], h_in), (sent[1], h_mid.at[pl.ds(1, 15)]), (sent[2], h_in)]
    for k in (4, 5, 3, 2, 6, 1, 7):
        s = lax.rem(seq + k, 8)
        src = h_all.at[pl.ds(pl.multiple_of(s * 16, 16), 16)]
        links.copy(src, h_in.at[k - 1], (s, dp), sent[0], got[0])

    def add_gram(i, gram):
        pieces = [t_all[i // 4, i % 4, u // 4, u % 4, h] for u in range(16) for h in range(2)]
        wide = jnp.concatenate(pieces, axis=1)
        return gram + dot(wide, wide, NT)

    gram = lax.fori_loop(0, 8, add_gram, jnp.zeros((128, 128), F32))
    fac[:, :128] = gram * d_row * d_col
    fac[:, 128:] = jnp.where(eye, 1.0, 0.0).astype(F32)
    links.wait(got[0], h_in)
    h_mid[0] = h_all[here] + jnp.sum(h_in[...], axis=0)
    for k in (10, 6, 9, 11, 14, 5, 7, 2, 8, 13, 15, 3, 4, 12, 1):
        links.copy(h_mid.at[0], h_mid.at[k], (seq, lax.rem(dp + k, 16)), sent[1], got[1])
    factor_steps(fac, 0, 8)
    links.wait(got[1], h_mid.at[pl.ds(1, 15)])
    h_out[here] = jnp.sum(h_mid[...], axis=0)
    for k in (4, 5, 3, 2, 6, 1, 7):
        links.copy(h_out.at[here], h_out.at[here], (lax.rem(seq + k, 8), dp), sent[2], got[2])
    factor_steps(fac, 8, 16)
    inverse = fac[:, 128:]
    panel = dot(inverse, pulled_t * d_col, precision=HIGHEST).T.astype(BF16)
    new_ref[...] = panel
    links.wait(got[2], h_in)
    ritz = dot(dot(inverse, h_out[...], precision=HIGHEST), inverse, NT, HIGHEST)

    mean = jnp.sum(jnp.where(eye, ritz, 0.0)) / 128
    shifted = ritz - jnp.where(eye, mean, 0.0)
    sign = shifted / (jnp.sqrt(jnp.sum(shifted * shifted)) + 1e-6)

    def split(a):
        high = a.astype(BF16)
        return high, (a - high.astype(F32)).astype(BF16)

    def product(a, b):
        return dot(a[0], b[0]) + (dot(a[0], b[1]) + dot(a[1], b[0]))

    def sweep(_, sign):
        parts = split(sign)
        square = product(parts, parts)
        return 0.5 * (3.0 * sign - product(split(square), parts))

    sign = lax.fori_loop(0, NS_STEPS, sweep, sign)
    positive = 0.5 * (shifted + dot(shifted, sign, precision=HIGHEST))
    positive_ref[...] = math.sqrt(32768) / mean * positive
    links.drain()


def finish(panel, positive, new_ref, sketch_ref):
    new_ref[...] = panel[...]
    sketch_ref[...] = dot(panel[...].astype(F32), positive[...], precision=HIGHEST)


def local(activations, start_panel):
    scratch = [
        pltpu.VMEM((256, 32768), BF16),
        pltpu.VMEM((2, 4, 4, 4, 2, 128, 128), BF16),
        pltpu.VMEM((2, 4, 4, 4, 2, 128, 128), BF16),
        pltpu.VMEM((256, 16384), BF16),
        pltpu.VMEM((128, 256), BF16),
        pltpu.VMEM((4, 4, 4, 2, 128, 128), BF16),
        pltpu.VMEM((128, 256), F32),
        pltpu.VMEM((128, 256), BF16),
        pltpu.VMEM((128, 128), F32),
        pltpu.VMEM((7, 16, 128), F32),
        pltpu.VMEM((16, 16, 128), F32),
        pltpu.VMEM((128, 128), F32),
    ]
    for parts in PARTS:
        for (_, rows), order in zip(parts, ORDERS):
            along_z = order[2] == "z"
            scratch += [
                pltpu.VMEM((2, 2, 4, rows, 128) if along_z else (2, 4, 2, rows, 128), BF16),
                pltpu.VMEM((2, 4, 4, rows, 128), BF16),
                pltpu.VMEM((4, 4, rows, 128), BF16),
                pltpu.VMEM((3, 4, rows, 128), BF16),
                pltpu.VMEM((4, rows, 128), BF16),
                pltpu.VMEM((3, rows, 128), BF16),
            ]
    scratch += [
        pltpu.SemaphoreType.DMA((10,)),
        pltpu.SemaphoreType.DMA((N_SEMS,)),
    ]
    panel, positive = pl.pallas_call(
        kernel,
        out_shape=(
            jax.ShapeDtypeStruct((256, 128), BF16),
            jax.ShapeDtypeStruct((128, 128), F32),
        ),
        in_specs=[pl.BlockSpec(memory_space=pl.ANY)] * 2,
        out_specs=(pl.BlockSpec(memory_space=pltpu.VMEM),) * 2,
        scratch_shapes=scratch,
        compiler_params=pltpu.CompilerParams(
            collective_id=0, has_side_effects=True, vmem_limit_bytes=60 << 20
        ),
        name="subspace",
    )(activations, start_panel)
    return pl.pallas_call(
        finish,
        out_shape=(
            jax.ShapeDtypeStruct((256, 128), BF16),
            jax.ShapeDtypeStruct((256, 128), F32),
        ),
        in_specs=[pl.BlockSpec(memory_space=pltpu.VMEM)] * 2,
        out_specs=(pl.BlockSpec(memory_space=pltpu.VMEM),) * 2,
        name="finish",
    )(panel, positive)


def solution(mesh):
    spec = P(("seq", "dp"), None)
    return jax.shard_map(
        local, mesh=mesh, in_specs=(spec, spec), out_specs=(spec, spec), check_vma=False
    )
```

```python
import math

import jax
import jax.numpy as jnp
from jax import lax
from jax.experimental import pallas as pl
from jax.experimental.pallas import tpu as pltpu
from jax.sharding import PartitionSpec as P

NS_STEPS = 12
MESH = pl.DeviceIdType.MESH
F32, BF16 = jnp.float32, jnp.bfloat16
HIGHEST = lax.Precision.HIGHEST
ORDERS = (("x", "y", "z"), ("z", "x", "y"), ("y", "z", "x"))
PARTS = (((0, 48), (48, 32), (80, 48)), ((0, 32), (32, 48), (80, 48)))
N_SEMS = 4 * 26 + 2 * 22 + 4 + 6


def dot(a, b, dims=(((1,), (0,)), ((), ())), precision=None):
    return lax.dot_general(a, b, dims, precision=precision, preferred_element_type=F32)


class Links:
    def __init__(self, sems, ruler):
        seq, dp = lax.axis_index("seq"), lax.axis_index("dp")
        x, y, z, c = dp % 4, dp // 4, seq // 2, seq % 2
        first = c == 0
        self.pos = dict(c=c, x=jnp.where(first, x, y), y=jnp.where(first, y, z), z=jnp.where(first, z, x))
        self.twin = dict(c=1 - c, x=jnp.where(first, y, x), y=jnp.where(first, z, y), z=jnp.where(first, x, z))
        self.seq, self.dp = seq, dp
        self.sems, self.ruler, self.used, self.sent = sems, ruler, 0, []

    def sem(self):
        self.used += 1
        return self.used - 1

    def at(self, axis, step):
        return lax.rem(self.pos[axis] + step, 4)

    def device(self, **other):
        p, first = {**self.pos, **other}, self.pos["c"] == 0
        x = jnp.where(first, p["x"], p["z"])
        y = jnp.where(first, p["y"], p["x"])
        z = jnp.where(first, p["z"], p["y"])
        return (z * 2 + p["c"], y * 4 + x)

    def columns(self, colour, apart=False):
        first = colour == 0
        wide, offset = (16, 0) if apart else (32, colour * 16)
        strides = [jnp.where(first, a, b) for a, b in ((wide, 1), (4, wide), (1, 4))]

        def columns(*where):
            place = offset + sum(i * stride for i, stride in zip(where, strides))
            return pl.ds(pl.multiple_of(place * 256, 256), 256)

        return columns

    def copy(self, src, dst, device, send, recv):
        pltpu.make_async_remote_copy(
            src_ref=src,
            dst_ref=dst,
            send_sem=self.sems.at[send],
            recv_sem=self.sems.at[recv],
            device_id=device,
            device_id_type=MESH,
        ).start()

    def wait(self, sem, like):
        pltpu.make_async_copy(like, like, self.sems.at[sem]).wait()

    def blocks(self, count):
        return self.ruler.at[pl.ds(0, 128), pl.ds(0, count * 128)]

    def drain(self):
        for sem, like in self.sent:
            self.wait(sem, like)


def gather(links, buf, parts, orders, handed, half=()):
    pos, every, three, two = links.pos, slice(None), pl.ds(0, 3), pl.ds(0, 2)
    halves = {1: pl.ds(0, 2), 3: pl.ds(2, 2)}
    other = links.device(c=1 - pos["c"])
    each = list(enumerate(zip(parts, orders)))

    def region(part, **index):
        p = {**pos, **index}
        return buf.at[(p["c"], p["z"], p["y"], p["x"], *half, pl.ds(*part), slice(None))]

    sends, first, early, late, last = [links.sem() for _ in range(5)]
    gets = [[first] + [links.sem() for _ in range(6)] + [last, early, late, links.sem()] for _ in orders]
    links.sent.append((sends, links.blocks(127)))
    handed[0].append((early, links.blocks(48)))
    handed[1].append((late, links.blocks(16)))
    rows = [[] for _ in orders]

    def send(o, get, axis, step, **index):
        src = region(parts[o], **index)
        links.copy(src, src, links.device(**{axis: links.at(axis, step)}), sends, gets[o][get])

    def wait(o, get, **size):
        links.wait(gets[o][get], region(parts[o], **size))

    def spread(o, row):
        a, b, c = orders[o]
        rows[o].append(row)
        for k in (1, 3):
            send(o, 2 + len(rows[o]), c, k, **row)

    def forward(o, j):
        a, b, c = orders[o]
        wait(o, 3 + j, **{a: every, c: two})
        for k in (1, 3):
            send(o, 10 if j == 3 else 7, c, k, **{**rows[o][j], a: halves[k], c: links.at(c, 4 - k)})

    def hand(o, step, **row):
        a, b, c = orders[o]
        src = region(parts[o], **{a: every, b: every, c: links.at(c, step), **row})
        links.copy(src, src, other, sends, gets[o][9 if step == 2 else 8])

    for o, (part, (a, b, c)) in each:
        for k in (2, 1, 3):
            send(o, 0, a, k)
    yield
    links.wait(first, links.blocks(3))
    for o, (part, (a, b, c)) in each:
        for k in (1, 3, 2):
            send(o, 2 if k == 2 else 1, b, k, **{a: every})
        spread(o, {a: every, b: pos[b]})
    yield
    for o, (part, (a, b, c)) in each:
        wait(o, 1, **{a: every, b: two})
        for step in (1, 3):
            spread(o, {a: every, b: links.at(b, 4 - step)})
    yield
    for o, _ in each:
        forward(o, 0)
    for o, (part, (a, b, c)) in each:
        wait(o, 2, **{a: every})
        spread(o, {a: every, b: links.at(b, 2)})
        hand(o, 0)
    yield
    for j in (1, 2, 3):
        for o, _ in each:
            forward(o, j)
    for k in (1, 3):
        for o, (part, (a, b, c)) in each:
            hand(o, 4 - k)
    yield
    links.wait(last, links.blocks(12))
    for o, (part, (a, b, c)) in each:
        for row in rows[o][:3]:
            hand(o, 2, **row)
    yield
    for o, (part, (a, b, c)) in each:
        wait(o, 10, **{a: every})
        hand(o, 2, **rows[o][3])


class Reduce:
    natural = ("z", "y", "x")
    steps = (2, 1, 3, 0)
    halves = {1: pl.ds(0, 2), 3: pl.ds(2, 2)}

    def __init__(self, links, work, h, bufs, parts, orders):
        self.links, self.work, self.h, self.bufs = links, work, h, bufs
        self.parts, self.orders = parts, orders
        self.each = list(enumerate(zip(parts, orders)))
        self.sends = links.sem()
        links.sent.append((self.sends, links.blocks(63)))
        self.gets = [[links.sem() for _ in range(4)] for _ in orders]
        self.plane_gets = [[self.gets[o][0]] + [links.sem() for _ in range(3)] for o in range(3)]
        two, three = pl.ds(0, 2), pl.ds(0, 3)
        self.sizes = []
        for o, (part, (c, b, a)) in self.each:
            sum1, sum2 = bufs[o][2], bufs[o][4]
            likes = (self.region(part, **{a: 0}), self.region(part, **{a: two}), sum1.at[three], sum2.at[three])
            self.sizes.append(likes)

    def at(self, part, **index):
        every = slice(None)
        where = [index.get(n, every) for n in self.natural]
        return (*where, self.h, pl.ds(*part), every)

    def region(self, part, **index):
        return self.work.at[self.at(part, **index)]

    def send(self, o, kind, src, dst, axis, to):
        links = self.links
        links.copy(src, dst, links.device(**{axis: to}), self.sends, self.gets[o][kind])

    def wait(self, o, kind):
        self.links.wait(self.gets[o][kind], self.sizes[o][kind])

    def start(self, n):
        links, z = self.links, self.links.at("z", self.steps[n])
        for o, (part, (c, b, a)) in self.each:
            via = self.bufs[o][0]
            left = "x" if a == "y" else "y"
            if a == "z" and n:
                continue
            for i, k in enumerate((1, 3)):
                src = self.region(part, **{"z": z, a: links.at(a, 2), left: self.halves[k]})
                dst = via.at[i] if a == "z" else via.at[i, z]
                to = links.device(**{a: links.at(a, k)})
                links.copy(src, dst, to, self.sends, self.plane_gets[o][n])

    def forward(self, n):
        links, work, z = self.links, self.work, self.links.at("z", self.steps[n])
        for o, (part, (c, b, a)) in self.each:
            if a == "z" and n:
                continue
            via, got = self.bufs[o][:2]
            like = {a: 0} if a == "z" else {a: 0, "z": 0}
            links.wait(self.plane_gets[o][n], self.region(part, **like))
            for i, k in enumerate((1, 3)):
                there = links.at(a, k)
                for j in range(2):
                    v = 2 * i + j
                    if a == "z":
                        blocks = [(dict(z=there, y=v, x=u), (i, j, u)) for u in range(4)]
                    else:
                        blocks = [(dict(z=z, y=there, x=v) if a == "y" else dict(z=z, y=v, x=there), (i, z, j))]
                    for block, piece in blocks:
                        where = self.at(part, **block)
                        work[where] = (work[where].astype(F32) + via[piece].astype(F32)).astype(BF16)
                index, dst = ({a: there}, got.at[i]) if a == "z" else ({a: there, "z": z}, got.at[i, z])
                self.send(o, 1, self.region(part, **index), dst, a, there)

    def own(self):
        links, pos = self.links, self.links.pos
        for o, (part, (c, b, a)) in self.each:
            got, sum1, got2 = self.bufs[o][1:4]
            self.wait(o, 1)
            left = [n for n in self.natural if n != a]
            lead = left.index(b) == 0
            for step in (2, 1, 3, 0):
                there = links.at(b, step)
                for w in range(4):
                    u, v = (there, w) if lead else (w, there)
                    mine = self.work[self.at(part, **{a: pos[a], left[0]: u, left[1]: v})].astype(F32)
                    sum1[u, v] = (mine + got[0, u, v].astype(F32) + got[1, u, v].astype(F32)).astype(BF16)
                if step:
                    src = sum1.at[there] if lead else sum1.at[:, there]
                    self.send(o, 2, src, got2.at[step - 1], b, there)

    def last_axis(self):
        links, pos = self.links, self.links.pos
        for o, (part, (c, b, a)) in self.each:
            sum1, got2, sum2, got3 = self.bufs[o][2:]
            self.wait(o, 2)
            lead = [n for n in self.natural if n != a].index(b) == 0
            for step in (2, 1, 3, 0):
                v = links.at(c, step)
                total = (sum1[pos[b], v] if lead else sum1[v, pos[b]]).astype(F32)
                for k in range(3):
                    total += got2[k, v].astype(F32)
                sum2[v] = total.astype(BF16)
                if step:
                    self.send(o, 3, sum2.at[v], got3.at[step - 1], c, v)

    def finish(self):
        totals = []
        for o, (part, (c, b, a)) in self.each:
            sum2, got3 = self.bufs[o][4:]
            self.wait(o, 3)
            total = sum2[self.links.pos[c]].astype(F32)
            for k in range(3):
                total += got3[k].astype(F32)
            totals.append(total)
        return jnp.concatenate(totals, axis=0)


def over_blocks(links, colour, near, body, state):
    columns = links.columns(colour)
    pos = {n: jnp.where(colour == links.pos["c"], links.pos[n], links.twin[n]) for n in "xyz"}
    pairs = [(dy, dx) for dy in range(4) for dx in range(4)]

    def visit(state, dz, pairs):
        blocks = []
        for dy, dx in pairs:
            where = [lax.rem(pos[n] + d, 4) for n, d in zip("zyx", (dz, dy, dx))]
            blocks.append((where, columns(*where)))
        return body(state, blocks)

    if not near:
        state = visit(state, 2, pairs)
    pairs = [p for p in pairs if (2 not in p) == near]
    return lax.fori_loop(0, 3, lambda i, state: visit(state, i + i // 2, pairs), state)


def gather_and_sum(links, gathers, handed, body, state):
    mine = links.pos["c"]
    state = over_blocks(links, mine, True, body(mine), state)
    for both in gathers:
        next(both)
    for sem, like in handed[0]:
        links.wait(sem, like)
    state = over_blocks(links, 1 - mine, True, body(1 - mine), state)
    for both in gathers:
        for _ in both:
            pass
    state = over_blocks(links, mine, False, body(mine), state)
    for sem, like in handed[1]:
        links.wait(sem, like)
    return over_blocks(links, 1 - mine, False, body(1 - mine), state)


def factor_steps(work, first, last):
    lane = lax.broadcasted_iota(jnp.int32, (8, 128), 1)
    row = lax.broadcasted_iota(jnp.int32, (8, 1), 0)

    def panel_step(p, _):
        start = pl.multiple_of(p * 8, 8)
        panel = work[pl.ds(start, 8), :]
        left = panel[:, :128]
        cols = [jnp.sum(jnp.where(lane == start + k, left, 0.0), axis=1, keepdims=True) for k in range(8)]
        scale = jnp.zeros((8, 1), F32)
        for k in range(8):
            pivot = cols[k][k : k + 1]
            scale = jnp.where(row == k, pivot, scale)
            below = jnp.where(row > k, cols[k] / pivot, 0.0)
            panel = panel - below * panel[k : k + 1]
            for m in range(k + 1, 8):
                cols[m] = cols[m] - below * cols[m][k : k + 1]
        panel = panel / jnp.sqrt(scale)
        work[pl.ds(start, 8), :] = panel
        rest = jnp.where(lane >= start + 8, panel[:, :128], 0.0)
        work[...] = work[...] - dot(rest, panel, (((0,), (0,)), ((), ())), HIGHEST)
        return _

    lax.fori_loop(first, last, panel_step, 0)


def kernel(act, start, new_ref, positive_ref, a_v, s_all, t_all, a_pair, proj_pair, work, fac, proj_t,
           h_all, h_in, h_mid, h_out, *rest):
    bufs = [[rest[18 * h + 6 * o : 18 * h + 6 * o + 6] for o in range(3)] for h in range(2)]
    local_sem, sems = rest[36:]
    links = Links(sems, a_v)
    pos = links.pos
    c, z, y, x = pos["c"], pos["z"], pos["y"], pos["x"]
    chunk = 4096

    load_s = []
    for h in range(2):
        rows = pl.ds(h * 128, 128)
        load_s.append(pltpu.make_async_copy(start.at[rows], s_all.at[c, z, y, x, h], local_sem.at[8 + h]))
        load_s[h].start()
    loads = []
    for i in range(8):
        cols = pl.ds(i * chunk, chunk)
        loads.append(pltpu.make_async_copy(act.at[:, cols], a_v.at[:, cols], local_sem.at[i]))
        loads[-1].start()

    barrier = pltpu.get_barrier_semaphore()
    near = [links.device(**{axis: links.at(axis, k)}) for axis in ("x", "y", "z") for k in (1, 2, 3)]
    near.append(links.device(c=1 - c))
    for device in near:
        pl.semaphore_signal(barrier, 1, device_id=device, device_id_type=MESH)
    pl.semaphore_wait(barrier, len(near))

    twin = links.device(c=1 - c)
    rows_sent, rows_got = links.sem(), links.sem()
    links.sent.append((rows_sent, a_pair))
    for i in range(4):
        src = act.at[:, pl.ds(pl.multiple_of((2 * i + 1 - c) * chunk, chunk), chunk)]
        links.copy(src, a_pair.at[:, pl.ds(i * chunk, chunk)], twin, rows_sent, rows_got)
    for load in load_s:
        load.wait()
    handed = [[], []]
    gathers = [gather(links, s_all, PARTS[h], ORDERS, handed, (h,)) for h in range(2)]
    for _ in range(5):
        next(gathers[0])
        next(gathers[1])
    for load in loads:
        load.wait()

    def project(colour):
        def body(total, blocks):
            pieces = [s_all[(colour, *where)].reshape(256, 128) for where, _ in blocks]
            wide = jnp.concatenate([a_v[:, cols] for _, cols in blocks], axis=1)
            return total + dot(wide, jnp.concatenate(pieces, axis=0))

        return body

    total = gather_and_sum(links, gathers, handed, project, jnp.zeros((256, 128), F32))
    proj_t[...] = total.T.astype(BF16)

    proj_sent, proj_got = links.sem(), links.sem()
    links.sent.append((proj_sent, proj_t))
    links.copy(proj_t, proj_pair, twin, proj_sent, proj_got)
    links.wait(rows_got, a_pair)
    links.wait(proj_got, proj_pair)
    columns, columns_pair = links.columns(c), links.columns(c, apart=True)

    proj_both = jnp.concatenate([proj_t[...], proj_pair[...]], axis=1)

    def plane(zz):
        for i in range(16):
            where = (zz, i // 4, i % 4)
            both = jnp.concatenate([a_v[:, columns(*where)], a_pair[:, columns_pair(*where)]], axis=0)
            piece = dot(proj_both, both)
            for h in range(2):
                work[(*where, h)] = piece[:, h * 128 : h * 128 + 128].astype(BF16)

    handed, pulled_t, gathers = [[], []], [None, None], [None, None]
    sums = [Reduce(links, work, h, bufs[h], PARTS[h], ORDERS) for h in range(2)]

    def done(h):
        pulled_t[h] = sums[h].finish()
        t_all[c, z, y, x, h] = pulled_t[h].astype(BF16)
        gathers[h] = gather(links, t_all, PARTS[h], ORDERS, handed, (h,))
        next(gathers[h])

    for n, step in enumerate(Reduce.steps):
        plane(links.at("z", step))
        sums[0].start(n)
    for n in range(4):
        sums[1].start(n)
    for n in range(4):
        sums[0].forward(n)
    for n in range(4):
        sums[1].forward(n)
    sums[0].own()
    sums[0].last_axis()
    sums[1].own()
    done(0)
    sums[1].last_axis()
    next(gathers[0])
    done(1)
    next(gathers[0])
    next(gathers[1])
    next(gathers[0])
    next(gathers[1])
    next(gathers[0])
    next(gathers[1])
    next(gathers[1])
    pulled_t = jnp.concatenate(pulled_t, axis=1)

    NT = (((1,), (1,)), ((), ()))

    def raw_and_squares(colour):
        def body(sums, blocks):
            raw, squares = sums
            halves = [t_all[(colour, *where, h)] for where, _ in blocks for h in range(2)]
            for half in halves:
                squares = squares + half.astype(F32) * half.astype(F32)
            wide = jnp.concatenate([a_v[:, cols] for _, cols in blocks], axis=1)
            return raw + dot(wide, jnp.concatenate(halves, axis=1), NT), squares

        return body

    zeros = (jnp.zeros((256, 128), F32), jnp.zeros((128, 128), F32))
    raw, squares = gather_and_sum(links, gathers, handed, raw_and_squares, zeros)

    rows = lax.broadcasted_iota(jnp.int32, (128, 128), 0)
    cols = lax.broadcasted_iota(jnp.int32, (128, 128), 1)
    eye = rows == cols
    d_col = 1.0 / jnp.sqrt(jnp.sum(squares, axis=1, keepdims=True))
    d_row = jnp.sum(jnp.where(eye, d_col, 0.0), axis=0, keepdims=True)
    raw = raw * d_row
    h_all[...] = dot(raw, raw, (((0,), (0,)), ((), ())), HIGHEST)

    seq, dp = links.seq, links.dp
    here = pl.ds(pl.multiple_of(seq * 16, 16), 16)
    sent, got = [links.sem() for _ in range(3)], [links.sem() for _ in range(3)]
    links.sent += [(sent[0], h_in), (sent[1], h_mid.at[pl.ds(1, 15)]), (sent[2], h_in)]
    for k in (4, 5, 3, 2, 6, 1, 7):
        s = lax.rem(seq + k, 8)
        src = h_all.at[pl.ds(pl.multiple_of(s * 16, 16), 16)]
        links.copy(src, h_in.at[k - 1], (s, dp), sent[0], got[0])

    def add_gram(i, gram):
        pieces = [t_all[i // 4, i % 4, u // 4, u % 4, h] for u in range(16) for h in range(2)]
        wide = jnp.concatenate(pieces, axis=1)
        return gram + dot(wide, wide, NT)

    gram = lax.fori_loop(0, 8, add_gram, jnp.zeros((128, 128), F32))
    fac[:, :128] = gram * d_row * d_col
    fac[:, 128:] = jnp.where(eye, 1.0, 0.0).astype(F32)
    links.wait(got[0], h_in)
    h_mid[0] = h_all[here] + jnp.sum(h_in[...], axis=0)
    for k in (10, 6, 9, 11, 14, 5, 7, 2, 8, 13, 15, 3, 4, 12, 1):
        links.copy(h_mid.at[0], h_mid.at[k], (seq, lax.rem(dp + k, 16)), sent[1], got[1])
    factor_steps(fac, 0, 10)
    links.wait(got[1], h_mid.at[pl.ds(1, 15)])
    h_out[here] = jnp.sum(h_mid[...], axis=0)
    for k in (4, 5, 3, 2, 6, 1, 7):
        links.copy(h_out.at[here], h_out.at[here], (lax.rem(seq + k, 8), dp), sent[2], got[2])
    factor_steps(fac, 10, 16)
    inverse = fac[:, 128:]
    panel = dot(inverse, pulled_t * d_col, precision=HIGHEST).T.astype(BF16)
    new_ref[...] = panel
    links.wait(got[2], h_in)
    ritz = dot(dot(inverse, h_out[...], precision=HIGHEST), inverse, NT, HIGHEST)

    mean = jnp.sum(jnp.where(eye, ritz, 0.0)) / 128
    shifted = ritz - jnp.where(eye, mean, 0.0)
    sign = shifted / (jnp.sqrt(jnp.sum(shifted * shifted)) + 1e-6)

    def split(a):
        high = a.astype(BF16)
        return high, (a - high.astype(F32)).astype(BF16)

    def product(a, b):
        return dot(a[0], b[0]) + (dot(a[0], b[1]) + dot(a[1], b[0]))

    def sweep(_, sign):
        parts = split(sign)
        square = product(parts, parts)
        return 0.5 * (3.0 * sign - product(split(square), parts))

    sign = lax.fori_loop(0, NS_STEPS, sweep, sign)
    positive = 0.5 * (shifted + dot(shifted, sign, precision=HIGHEST))
    positive_ref[...] = math.sqrt(32768) / mean * positive
    links.drain()


def finish(panel, positive, new_ref, sketch_ref):
    new_ref[...] = panel[...]
    sketch_ref[...] = dot(panel[...].astype(F32), positive[...], precision=HIGHEST)


def local(activations, start_panel):
    scratch = [
        pltpu.VMEM((256, 32768), BF16),
        pltpu.VMEM((2, 4, 4, 4, 2, 128, 128), BF16),
        pltpu.VMEM((2, 4, 4, 4, 2, 128, 128), BF16),
        pltpu.VMEM((256, 16384), BF16),
        pltpu.VMEM((128, 256), BF16),
        pltpu.VMEM((4, 4, 4, 2, 128, 128), BF16),
        pltpu.VMEM((128, 256), F32),
        pltpu.VMEM((128, 256), BF16),
        pltpu.VMEM((128, 128), F32),
        pltpu.VMEM((7, 16, 128), F32),
        pltpu.VMEM((16, 16, 128), F32),
        pltpu.VMEM((128, 128), F32),
    ]
    for parts in PARTS:
        for (_, rows), order in zip(parts, ORDERS):
            along_z = order[2] == "z"
            scratch += [
                pltpu.VMEM((2, 2, 4, rows, 128) if along_z else (2, 4, 2, rows, 128), BF16),
                pltpu.VMEM((2, 4, 4, rows, 128), BF16),
                pltpu.VMEM((4, 4, rows, 128), BF16),
                pltpu.VMEM((3, 4, rows, 128), BF16),
                pltpu.VMEM((4, rows, 128), BF16),
                pltpu.VMEM((3, rows, 128), BF16),
            ]
    scratch += [
        pltpu.SemaphoreType.DMA((10,)),
        pltpu.SemaphoreType.DMA((N_SEMS,)),
    ]
    panel, positive = pl.pallas_call(
        kernel,
        out_shape=(
            jax.ShapeDtypeStruct((256, 128), BF16),
            jax.ShapeDtypeStruct((128, 128), F32),
        ),
        in_specs=[pl.BlockSpec(memory_space=pl.ANY)] * 2,
        out_specs=(pl.BlockSpec(memory_space=pltpu.VMEM),) * 2,
        scratch_shapes=scratch,
        compiler_params=pltpu.CompilerParams(
            collective_id=0, has_side_effects=True, vmem_limit_bytes=60 << 20
        ),
        name="subspace",
    )(activations, start_panel)
    return pl.pallas_call(
        finish,
        out_shape=(
            jax.ShapeDtypeStruct((256, 128), BF16),
            jax.ShapeDtypeStruct((256, 128), F32),
        ),
        in_specs=[pl.BlockSpec(memory_space=pltpu.VMEM)] * 2,
        out_specs=(pl.BlockSpec(memory_space=pltpu.VMEM),) * 2,
        name="finish",
    )(panel, positive)


def solution(mesh):
    spec = P(("seq", "dp"), None)
    return jax.shard_map(
        local, mesh=mesh, in_specs=(spec, spec), out_specs=(spec, spec), check_vma=False
    )
```

```python
import math

import jax
import jax.numpy as jnp
from jax import lax
from jax.experimental import pallas as pl
from jax.experimental.pallas import tpu as pltpu
from jax.sharding import PartitionSpec as P

NS_STEPS = 12
MESH = pl.DeviceIdType.MESH
F32, BF16 = jnp.float32, jnp.bfloat16
HIGHEST = lax.Precision.HIGHEST
ORDERS = (("x", "y", "z"), ("z", "x", "y"), ("y", "z", "x"))
PARTS = (((0, 48), (48, 32), (80, 48)), ((0, 32), (32, 48), (80, 48)))
N_SEMS = 4 * 12 + 2 * 22 + 4 + 6


def dot(a, b, dims=(((1,), (0,)), ((), ())), precision=None):
    return lax.dot_general(a, b, dims, precision=precision, preferred_element_type=F32)


class Links:
    def __init__(self, sems, ruler):
        seq, dp = lax.axis_index("seq"), lax.axis_index("dp")
        x, y, z, c = dp % 4, dp // 4, seq // 2, seq % 2
        first = c == 0
        self.pos = dict(c=c, x=jnp.where(first, x, y), y=jnp.where(first, y, z), z=jnp.where(first, z, x))
        self.twin = dict(c=1 - c, x=jnp.where(first, y, x), y=jnp.where(first, z, y), z=jnp.where(first, x, z))
        self.seq, self.dp = seq, dp
        self.sems, self.ruler, self.used, self.sent = sems, ruler, 0, []

    def sem(self):
        self.used += 1
        return self.used - 1

    def at(self, axis, step):
        return lax.rem(self.pos[axis] + step, 4)

    def device(self, **other):
        p, first = {**self.pos, **other}, self.pos["c"] == 0
        x = jnp.where(first, p["x"], p["z"])
        y = jnp.where(first, p["y"], p["x"])
        z = jnp.where(first, p["z"], p["y"])
        return (z * 2 + p["c"], y * 4 + x)

    def columns(self, colour, apart=False):
        first = colour == 0
        wide, offset = (16, 0) if apart else (32, colour * 16)
        strides = [jnp.where(first, a, b) for a, b in ((wide, 1), (4, wide), (1, 4))]

        def columns(*where):
            place = offset + sum(i * stride for i, stride in zip(where, strides))
            return pl.ds(pl.multiple_of(place * 256, 256), 256)

        return columns

    def copy(self, src, dst, device, send, recv):
        pltpu.make_async_remote_copy(
            src_ref=src,
            dst_ref=dst,
            send_sem=self.sems.at[send],
            recv_sem=self.sems.at[recv],
            device_id=device,
            device_id_type=MESH,
        ).start()

    def wait(self, sem, like):
        pltpu.make_async_copy(like, like, self.sems.at[sem]).wait()

    def blocks(self, count):
        return self.ruler.at[pl.ds(0, 128), pl.ds(0, count * 128)]

    def drain(self):
        for sem, like in self.sent:
            self.wait(sem, like)


def gather(links, buf, parts, orders, handed, half=()):
    pos, every, three, two = links.pos, slice(None), pl.ds(0, 3), pl.ds(0, 2)
    halves = {1: pl.ds(0, 2), 3: pl.ds(2, 2)}
    other = links.device(c=1 - pos["c"])
    each = list(enumerate(zip(parts, orders)))

    def region(part, **index):
        p = {**pos, **index}
        return buf.at[(p["c"], p["z"], p["y"], p["x"], *half, pl.ds(*part), slice(None))]

    sends, first, early, late, last = [links.sem() for _ in range(5)]
    near, far, *third = [links.sem() for _ in range(6)]
    final = links.sem()
    gets = [[first, near, far, *third, last, early, late, final] for _ in orders]
    links.sent.append((sends, links.blocks(127)))
    handed[0].append((early, links.blocks(48)))
    handed[1].append((late, links.blocks(16)))
    rows = [[] for _ in orders]

    def send(o, get, axis, step, **index):
        src = region(parts[o], **index)
        links.copy(src, src, links.device(**{axis: links.at(axis, step)}), sends, gets[o][get])

    def spread(o, row):
        a, b, c = orders[o]
        rows[o].append(row)
        for k in (1, 3):
            send(o, 2 + len(rows[o]), c, k, **row)

    def forward(o, j):
        a, b, c = orders[o]
        for k in (1, 3):
            send(o, 10 if j == 3 else 7, c, k, **{**rows[o][j], a: halves[k], c: links.at(c, 4 - k)})

    def hand(o, step, **row):
        a, b, c = orders[o]
        src = region(parts[o], **{a: every, b: every, c: links.at(c, step), **row})
        links.copy(src, src, other, sends, gets[o][9 if step == 2 else 8])

    for o, (part, (a, b, c)) in each:
        for k in (2, 1, 3):
            send(o, 0, a, k)
    yield
    links.wait(first, links.blocks(3))
    for o, (part, (a, b, c)) in each:
        for k in (1, 3, 2):
            send(o, 2 if k == 2 else 1, b, k, **{a: every})
    for o, (part, (a, b, c)) in each:
        spread(o, {a: every, b: pos[b]})
    yield
    links.wait(near, links.blocks(8))
    for o, (part, (a, b, c)) in each:
        for step in (1, 3):
            spread(o, {a: every, b: links.at(b, 4 - step)})
    yield
    links.wait(third[0], links.blocks(8))
    for o, _ in each:
        forward(o, 0)
    links.wait(far, links.blocks(4))
    for o, (part, (a, b, c)) in each:
        spread(o, {a: every, b: links.at(b, 2)})
        hand(o, 0)
    yield
    for j in (1, 2, 3):
        links.wait(third[j], links.blocks(8))
        for o, _ in each:
            forward(o, j)
    for k in (1, 3):
        for o, (part, (a, b, c)) in each:
            hand(o, 4 - k)
    yield
    links.wait(last, links.blocks(12))
    for o, (part, (a, b, c)) in each:
        for row in rows[o][:3]:
            hand(o, 2, **row)
    yield
    links.wait(final, links.blocks(4))
    for o, (part, (a, b, c)) in each:
        hand(o, 2, **rows[o][3])


class Reduce:
    natural = ("z", "y", "x")
    steps = (2, 1, 3, 0)
    halves = {1: pl.ds(0, 2), 3: pl.ds(2, 2)}

    def __init__(self, links, work, h, bufs, parts, orders):
        self.links, self.work, self.h, self.bufs = links, work, h, bufs
        self.parts, self.orders = parts, orders
        self.each = list(enumerate(zip(parts, orders)))
        self.sends = links.sem()
        links.sent.append((self.sends, links.blocks(63)))
        self.gets = [[links.sem() for _ in range(4)] for _ in orders]
        self.plane_gets = [[self.gets[o][0]] + [links.sem() for _ in range(3)] for o in range(3)]
        two, three = pl.ds(0, 2), pl.ds(0, 3)
        self.sizes = []
        for o, (part, (c, b, a)) in self.each:
            sum1, sum2 = bufs[o][2], bufs[o][4]
            likes = (self.region(part, **{a: 0}), self.region(part, **{a: two}), sum1.at[three], sum2.at[three])
            self.sizes.append(likes)

    def at(self, part, **index):
        every = slice(None)
        where = [index.get(n, every) for n in self.natural]
        return (*where, self.h, pl.ds(*part), every)

    def region(self, part, **index):
        return self.work.at[self.at(part, **index)]

    def send(self, o, kind, src, dst, axis, to):
        links = self.links
        links.copy(src, dst, links.device(**{axis: to}), self.sends, self.gets[o][kind])

    def wait(self, o, kind):
        self.links.wait(self.gets[o][kind], self.sizes[o][kind])

    def start(self, n):
        links, z = self.links, self.links.at("z", self.steps[n])
        for o, (part, (c, b, a)) in self.each:
            via = self.bufs[o][0]
            left = "x" if a == "y" else "y"
            if a == "z" and n:
                continue
            for i, k in enumerate((1, 3)):
                src = self.region(part, **{"z": z, a: links.at(a, 2), left: self.halves[k]})
                dst = via.at[i] if a == "z" else via.at[i, z]
                to = links.device(**{a: links.at(a, k)})
                links.copy(src, dst, to, self.sends, self.plane_gets[o][n])

    def forward(self, n):
        links, work, z = self.links, self.work, self.links.at("z", self.steps[n])
        for o, (part, (c, b, a)) in self.each:
            if a == "z" and n:
                continue
            via, got = self.bufs[o][:2]
            like = {a: 0} if a == "z" else {a: 0, "z": 0}
            links.wait(self.plane_gets[o][n], self.region(part, **like))
            for i, k in enumerate((1, 3)):
                there = links.at(a, k)
                for j in range(2):
                    v = 2 * i + j
                    if a == "z":
                        blocks = [(dict(z=there, y=v, x=u), (i, j, u)) for u in range(4)]
                    else:
                        blocks = [(dict(z=z, y=there, x=v) if a == "y" else dict(z=z, y=v, x=there), (i, z, j))]
                    for block, piece in blocks:
                        where = self.at(part, **block)
                        work[where] = (work[where].astype(F32) + via[piece].astype(F32)).astype(BF16)
                index, dst = ({a: there}, got.at[i]) if a == "z" else ({a: there, "z": z}, got.at[i, z])
                self.send(o, 1, self.region(part, **index), dst, a, there)

    def own(self):
        links, pos = self.links, self.links.pos
        for o, (part, (c, b, a)) in self.each:
            got, sum1, got2 = self.bufs[o][1:4]
            self.wait(o, 1)
            left = [n for n in self.natural if n != a]
            lead = left.index(b) == 0
            for step in (2, 1, 3, 0):
                there = links.at(b, step)
                for w in range(4):
                    u, v = (there, w) if lead else (w, there)
                    mine = self.work[self.at(part, **{a: pos[a], left[0]: u, left[1]: v})].astype(F32)
                    sum1[u, v] = (mine + got[0, u, v].astype(F32) + got[1, u, v].astype(F32)).astype(BF16)
                if step:
                    src = sum1.at[there] if lead else sum1.at[:, there]
                    self.send(o, 2, src, got2.at[step - 1], b, there)

    def last_axis(self):
        links, pos = self.links, self.links.pos
        for o, (part, (c, b, a)) in self.each:
            sum1, got2, sum2, got3 = self.bufs[o][2:]
            self.wait(o, 2)
            lead = [n for n in self.natural if n != a].index(b) == 0
            for step in (2, 1, 3, 0):
                v = links.at(c, step)
                total = (sum1[pos[b], v] if lead else sum1[v, pos[b]]).astype(F32)
                for k in range(3):
                    total += got2[k, v].astype(F32)
                sum2[v] = total.astype(BF16)
                if step:
                    self.send(o, 3, sum2.at[v], got3.at[step - 1], c, v)

    def finish(self):
        totals = []
        for o, (part, (c, b, a)) in self.each:
            sum2, got3 = self.bufs[o][4:]
            self.wait(o, 3)
            total = sum2[self.links.pos[c]].astype(F32)
            for k in range(3):
                total += got3[k].astype(F32)
            totals.append(total)
        return jnp.concatenate(totals, axis=0)


def over_blocks(links, colour, near, body, state):
    columns = links.columns(colour)
    pos = {n: jnp.where(colour == links.pos["c"], links.pos[n], links.twin[n]) for n in "xyz"}
    pairs = [(dy, dx) for dy in range(4) for dx in range(4)]

    def visit(state, dz, pairs):
        blocks = []
        for dy, dx in pairs:
            where = [lax.rem(pos[n] + d, 4) for n, d in zip("zyx", (dz, dy, dx))]
            blocks.append((where, columns(*where)))
        return body(state, blocks)

    if not near:
        state = visit(state, 2, pairs)
    pairs = [p for p in pairs if (2 not in p) == near]
    return lax.fori_loop(0, 3, lambda i, state: visit(state, i + i // 2, pairs), state)


def gather_and_sum(links, gathers, handed, body, state):
    mine = links.pos["c"]
    state = over_blocks(links, mine, True, body(mine), state)
    for both in gathers:
        next(both)
    for sem, like in handed[0]:
        links.wait(sem, like)
    state = over_blocks(links, 1 - mine, True, body(1 - mine), state)
    for both in gathers:
        for _ in both:
            pass
    state = over_blocks(links, mine, False, body(mine), state)
    for sem, like in handed[1]:
        links.wait(sem, like)
    return over_blocks(links, 1 - mine, False, body(1 - mine), state)


def factor_steps(work, first, last):
    lane = lax.broadcasted_iota(jnp.int32, (8, 128), 1)
    row = lax.broadcasted_iota(jnp.int32, (8, 1), 0)

    def panel_step(p, _):
        start = pl.multiple_of(p * 8, 8)
        panel = work[pl.ds(start, 8), :]
        left = panel[:, :128]
        cols = [jnp.sum(jnp.where(lane == start + k, left, 0.0), axis=1, keepdims=True) for k in range(8)]
        scale = jnp.zeros((8, 1), F32)
        for k in range(8):
            pivot = cols[k][k : k + 1]
            scale = jnp.where(row == k, pivot, scale)
            below = jnp.where(row > k, cols[k] / pivot, 0.0)
            panel = panel - below * panel[k : k + 1]
            for m in range(k + 1, 8):
                cols[m] = cols[m] - below * cols[m][k : k + 1]
        panel = panel / jnp.sqrt(scale)
        work[pl.ds(start, 8), :] = panel
        rest = jnp.where(lane >= start + 8, panel[:, :128], 0.0)
        work[...] = work[...] - dot(rest, panel, (((0,), (0,)), ((), ())), HIGHEST)
        return _

    lax.fori_loop(first, last, panel_step, 0)


def kernel(act, start, new_ref, positive_ref, a_v, s_all, t_all, a_pair, proj_pair, work, fac, proj_t,
           h_all, h_in, h_mid, h_out, *rest):
    bufs = [[rest[18 * h + 6 * o : 18 * h + 6 * o + 6] for o in range(3)] for h in range(2)]
    local_sem, sems = rest[36:]
    links = Links(sems, a_v)
    pos = links.pos
    c, z, y, x = pos["c"], pos["z"], pos["y"], pos["x"]
    chunk = 4096

    load_s = []
    for h in range(2):
        rows = pl.ds(h * 128, 128)
        load_s.append(pltpu.make_async_copy(start.at[rows], s_all.at[c, z, y, x, h], local_sem.at[8 + h]))
        load_s[h].start()
    loads = []
    for i in range(8):
        cols = pl.ds(i * chunk, chunk)
        loads.append(pltpu.make_async_copy(act.at[:, cols], a_v.at[:, cols], local_sem.at[i]))
        loads[-1].start()

    barrier = pltpu.get_barrier_semaphore()
    near = [links.device(**{axis: links.at(axis, k)}) for axis in ("x", "y", "z") for k in (1, 2, 3)]
    near.append(links.device(c=1 - c))
    for device in near:
        pl.semaphore_signal(barrier, 1, device_id=device, device_id_type=MESH)
    pl.semaphore_wait(barrier, len(near))

    for load in load_s:
        load.wait()
    handed = [[], []]
    gathers = [gather(links, s_all, PARTS[h], ORDERS, handed, (h,)) for h in range(2)]
    next(gathers[0])
    next(gathers[1])
    twin = links.device(c=1 - c)
    rows_sent, rows_got = links.sem(), links.sem()
    links.sent.append((rows_sent, a_pair))
    for i in range(4):
        src = act.at[:, pl.ds(pl.multiple_of((2 * i + 1 - c) * chunk, chunk), chunk)]
        links.copy(src, a_pair.at[:, pl.ds(i * chunk, chunk)], twin, rows_sent, rows_got)
    for _ in range(4):
        next(gathers[0])
        next(gathers[1])
    for load in loads:
        load.wait()

    def project(colour):
        def body(total, blocks):
            pieces = [s_all[(colour, *where)].reshape(256, 128) for where, _ in blocks]
            wide = jnp.concatenate([a_v[:, cols] for _, cols in blocks], axis=1)
            return total + dot(wide, jnp.concatenate(pieces, axis=0))

        return body

    total = gather_and_sum(links, gathers, handed, project, jnp.zeros((256, 128), F32))
    proj_t[...] = total.T.astype(BF16)

    proj_sent, proj_got = links.sem(), links.sem()
    links.sent.append((proj_sent, proj_t))
    links.copy(proj_t, proj_pair, twin, proj_sent, proj_got)
    links.wait(rows_got, a_pair)
    links.wait(proj_got, proj_pair)
    columns, columns_pair = links.columns(c), links.columns(c, apart=True)

    proj_both = jnp.concatenate([proj_t[...], proj_pair[...]], axis=1)

    def plane(zz):
        for i in range(16):
            where = (zz, i // 4, i % 4)
            both = jnp.concatenate([a_v[:, columns(*where)], a_pair[:, columns_pair(*where)]], axis=0)
            piece = dot(proj_both, both)
            for h in range(2):
                work[(*where, h)] = piece[:, h * 128 : h * 128 + 128].astype(BF16)

    handed, pulled_t, gathers = [[], []], [None, None], [None, None]
    sums = [Reduce(links, work, h, bufs[h], PARTS[h], ORDERS) for h in range(2)]

    def done(h):
        pulled_t[h] = sums[h].finish()
        t_all[c, z, y, x, h] = pulled_t[h].astype(BF16)
        gathers[h] = gather(links, t_all, PARTS[h], ORDERS, handed, (h,))
        next(gathers[h])

    for n, step in enumerate(Reduce.steps):
        plane(links.at("z", step))
        sums[0].start(n)
    for n in range(4):
        sums[1].start(n)
    for n in range(4):
        sums[0].forward(n)
    for n in range(4):
        sums[1].forward(n)
    sums[0].own()
    sums[0].last_axis()
    sums[1].own()
    done(0)
    sums[1].last_axis()
    next(gathers[0])
    done(1)
    next(gathers[0])
    next(gathers[1])
    next(gathers[0])
    next(gathers[1])
    next(gathers[0])
    next(gathers[1])
    next(gathers[1])
    pulled_t = jnp.concatenate(pulled_t, axis=1)

    NT = (((1,), (1,)), ((), ()))

    def raw_and_squares(colour):
        def body(sums, blocks):
            raw, squares = sums
            halves = [t_all[(colour, *where, h)] for where, _ in blocks for h in range(2)]
            for half in halves:
                squares = squares + half.astype(F32) * half.astype(F32)
            wide = jnp.concatenate([a_v[:, cols] for _, cols in blocks], axis=1)
            return raw + dot(wide, jnp.concatenate(halves, axis=1), NT), squares

        return body

    zeros = (jnp.zeros((256, 128), F32), jnp.zeros((128, 128), F32))
    raw, squares = gather_and_sum(links, gathers, handed, raw_and_squares, zeros)

    rows = lax.broadcasted_iota(jnp.int32, (128, 128), 0)
    cols = lax.broadcasted_iota(jnp.int32, (128, 128), 1)
    eye = rows == cols
    d_col = 1.0 / jnp.sqrt(jnp.sum(squares, axis=1, keepdims=True))
    d_row = jnp.sum(jnp.where(eye, d_col, 0.0), axis=0, keepdims=True)
    raw = raw * d_row
    h_all[...] = dot(raw, raw, (((0,), (0,)), ((), ())), HIGHEST)

    seq, dp = links.seq, links.dp
    here = pl.ds(pl.multiple_of(seq * 16, 16), 16)
    sent, got = [links.sem() for _ in range(3)], [links.sem() for _ in range(3)]
    links.sent += [(sent[0], h_in), (sent[1], h_mid.at[pl.ds(1, 15)]), (sent[2], h_in)]
    for k in (4, 5, 3, 2, 6, 1, 7):
        s = lax.rem(seq + k, 8)
        src = h_all.at[pl.ds(pl.multiple_of(s * 16, 16), 16)]
        links.copy(src, h_in.at[k - 1], (s, dp), sent[0], got[0])

    def add_gram(i, gram):
        pieces = [t_all[i // 4, i % 4, u // 4, u % 4, h] for u in range(16) for h in range(2)]
        wide = jnp.concatenate(pieces, axis=1)
        return gram + dot(wide, wide, NT)

    gram = lax.fori_loop(0, 8, add_gram, jnp.zeros((128, 128), F32))
    fac[:, :128] = gram * d_row * d_col
    fac[:, 128:] = jnp.where(eye, 1.0, 0.0).astype(F32)
    links.wait(got[0], h_in)
    h_mid[0] = h_all[here] + jnp.sum(h_in[...], axis=0)
    for k in (10, 6, 9, 11, 14, 5, 7, 2, 8, 13, 15, 3, 4, 12, 1):
        links.copy(h_mid.at[0], h_mid.at[k], (seq, lax.rem(dp + k, 16)), sent[1], got[1])
    factor_steps(fac, 0, 10)
    links.wait(got[1], h_mid.at[pl.ds(1, 15)])
    h_out[here] = jnp.sum(h_mid[...], axis=0)
    for k in (4, 5, 3, 2, 6, 1, 7):
        links.copy(h_out.at[here], h_out.at[here], (lax.rem(seq + k, 8), dp), sent[2], got[2])
    factor_steps(fac, 10, 16)
    inverse = fac[:, 128:]
    panel = dot(inverse, pulled_t * d_col, precision=HIGHEST).T.astype(BF16)
    new_ref[...] = panel
    links.wait(got[2], h_in)
    ritz = dot(dot(inverse, h_out[...], precision=HIGHEST), inverse, NT, HIGHEST)

    mean = jnp.sum(jnp.where(eye, ritz, 0.0)) / 128
    shifted = ritz - jnp.where(eye, mean, 0.0)
    sign = shifted / (jnp.sqrt(jnp.sum(shifted * shifted)) + 1e-6)

    def split(a):
        high = a.astype(BF16)
        return high, (a - high.astype(F32)).astype(BF16)

    def product(a, b):
        return dot(a[0], b[0]) + (dot(a[0], b[1]) + dot(a[1], b[0]))

    def sweep(_, sign):
        parts = split(sign)
        square = product(parts, parts)
        return 0.5 * (3.0 * sign - product(split(square), parts))

    sign = lax.fori_loop(0, NS_STEPS, sweep, sign)
    positive = 0.5 * (shifted + dot(shifted, sign, precision=HIGHEST))
    positive_ref[...] = math.sqrt(32768) / mean * positive
    links.drain()


def finish(panel, positive, new_ref, sketch_ref):
    new_ref[...] = panel[...]
    sketch_ref[...] = dot(panel[...].astype(F32), positive[...], precision=HIGHEST)


def local(activations, start_panel):
    scratch = [
        pltpu.VMEM((256, 32768), BF16),
        pltpu.VMEM((2, 4, 4, 4, 2, 128, 128), BF16),
        pltpu.VMEM((2, 4, 4, 4, 2, 128, 128), BF16),
        pltpu.VMEM((256, 16384), BF16),
        pltpu.VMEM((128, 256), BF16),
        pltpu.VMEM((4, 4, 4, 2, 128, 128), BF16),
        pltpu.VMEM((128, 256), F32),
        pltpu.VMEM((128, 256), BF16),
        pltpu.VMEM((128, 128), F32),
        pltpu.VMEM((7, 16, 128), F32),
        pltpu.VMEM((16, 16, 128), F32),
        pltpu.VMEM((128, 128), F32),
    ]
    for parts in PARTS:
        for (_, rows), order in zip(parts, ORDERS):
            along_z = order[2] == "z"
            scratch += [
                pltpu.VMEM((2, 2, 4, rows, 128) if along_z else (2, 4, 2, rows, 128), BF16),
                pltpu.VMEM((2, 4, 4, rows, 128), BF16),
                pltpu.VMEM((4, 4, rows, 128), BF16),
                pltpu.VMEM((3, 4, rows, 128), BF16),
                pltpu.VMEM((4, rows, 128), BF16),
                pltpu.VMEM((3, rows, 128), BF16),
            ]
    scratch += [
        pltpu.SemaphoreType.DMA((10,)),
        pltpu.SemaphoreType.DMA((N_SEMS,)),
    ]
    panel, positive = pl.pallas_call(
        kernel,
        out_shape=(
            jax.ShapeDtypeStruct((256, 128), BF16),
            jax.ShapeDtypeStruct((128, 128), F32),
        ),
        in_specs=[pl.BlockSpec(memory_space=pl.ANY)] * 2,
        out_specs=(pl.BlockSpec(memory_space=pltpu.VMEM),) * 2,
        scratch_shapes=scratch,
        compiler_params=pltpu.CompilerParams(
            collective_id=0, has_side_effects=True, vmem_limit_bytes=60 << 20
        ),
        name="subspace",
    )(activations, start_panel)
    return pl.pallas_call(
        finish,
        out_shape=(
            jax.ShapeDtypeStruct((256, 128), BF16),
            jax.ShapeDtypeStruct((256, 128), F32),
        ),
        in_specs=[pl.BlockSpec(memory_space=pltpu.VMEM)] * 2,
        out_specs=(pl.BlockSpec(memory_space=pltpu.VMEM),) * 2,
        name="finish",
    )(panel, positive)


def solution(mesh):
    spec = P(("seq", "dp"), None)
    return jax.shard_map(
        local, mesh=mesh, in_specs=(spec, spec), out_specs=(spec, spec), check_vma=False
    )
```
